32 devices in a mesh: group: 2 (over y), tile: 4 (over z), view: 2 (over x), sub: 2 (over core).
Axes of the slice: x: 2, y: 2, z: 4, core: 2. Of those that a mesh axis runs over, the one named last changes fastest.
Arguments:
- centers: float32 [3, 131072], P(None, ('group', 'tile', 'view', 'sub')), parts along dimension 1, may hold values from -2 to 2
- scale_log: float32 [3, 131072], P(None, ('group', 'tile', 'view', 'sub')), parts along dimension 1, may hold values from -6.2 to -3.9
- shear_terms: float32 [3, 131072], P(None, ('group', 'tile', 'view', 'sub')), parts along dimension 1, may hold values from -3 to 3
- opacity_logit: float32 [131072], P(('group', 'tile', 'view', 'sub')), parts along dimension 0, may hold values from -7 to -2
- sh_coeffs: float32 [48, 131072], P(None, ('group', 'tile', 'view', 'sub')), parts along dimension 1, may hold values from -3 to 3
- cameras: float32 [4, 8], P('group'), parts along dimension 0, may hold values from -100 to 600, as said below
- appearance: float32 [4, 12], P(('group', 'view')), parts along dimension 0, may hold values from -1 to 1
- target: float32 [3, 4, 8, 8, 256], P(None, ('group', 'view'), ('tile', 'sub')), parts along dimension 1, may hold values from 0 to 1
- send_index: int32 [32, 16, 256], P(('group', 'tile', 'view', 'sub')), parts along dimension 0, may hold values from 0 to 4095, as said below
- send_count: int32 [32, 16], P(('group', 'tile', 'view', 'sub')), parts along dimension 0, may hold values from 1 to 256, as said below
- tile_list: int32 [32, 8, 512], P(('group', 'tile', 'view', 'sub')), parts along dimension 0, may hold values from 0 to 4095, as said below
- tile_count: int32 [32, 8], P(('group', 'tile', 'view', 'sub')), parts along dimension 0, may hold values from 1 to 512
Outputs:
- rendered: float32 [3, 4, 8, 8, 256], P(None, ('group', 'view'), ('tile', 'sub')), parts along dimension 1
- param_grad: float32 [58, 131072], P(None, ('group', 'tile', 'view', 'sub')), parts along dimension 1
- appearance_grad: float32 [4, 12], P(('group', 'view')), parts along dimension 0
The draws below stay inside these ranges and needn't reach their ends.
There are 2 independent parts, one for each index of `group`. The reference program is written for one: setup_inputs(seed, part) draws one part's arguments, and reference() takes and returns one part's arrays. A program takes and returns all parts, laid end to end along the dimension named above; each array names one. Nothing has to cross between parts.
Inputs may be any that keep to these rules, and one draw needn't show every extreme that they name: `send_index`: the 16 x 256 slots of device s name each of its Gaussians once, so a Gaussian is sent to at most one device; slots j >= send_count[s, d] are unused. `send_count`: some device receives 256 rows from every device. `tile_list`: live entries index the device's pool; every pool item stands in exactly one list; empty entries are 0. `cameras`: columns fx, sx, cx, fy, sy, cy, polar, azimuth; fx and fy lie in 300 to 600.
All inputs are finite; a program needn't handle non-finite values.
Results may differ from the reference program's by a relative error of at most 0.0003.
Values sent between devices are 32-bit elements; how exact they have to be, the bound alone decides.
A program may use at most 128 MiB of HBM per device.

```python
import math
import jax
import jax.numpy as jnp
from jax import lax

K = 512
TCOLS = 8
TILE_PIX = 256
SH_COEF = 48
NDEV = 16
G_DEV = 4096
CAP = 256
GAUSS = 65536
VIEWS = 2
SUB_ROWS = 2
ROWS = 8
N_TILE = 4
N_VIEW = 2
N_SUB = 2


def route_plan(key):
    key = jax.random.fold_in(key, 11)
    key_shift, key_full, key_count, key_order, key_tiles = jax.random.split(key, 5)
    shifts = jax.random.randint(key_shift, (NDEV,), 0, 4)
    full_dest = jax.random.randint(key_full, (), 0, NDEV)
    dest_load = jnp.maximum(jnp.right_shift(jnp.full((NDEV,), CAP, jnp.int32), shifts), 1)
    least = jnp.maximum(dest_load // 2, 1)
    counts = jax.random.randint(key_count, (NDEV, NDEV), least[None, :], dest_load[None, :] + 1)
    counts = jnp.where(jnp.arange(NDEV)[None, :] == full_dest, CAP, counts).astype(jnp.int32)
    orders = jax.vmap(lambda sub_key: jax.random.permutation(sub_key, G_DEV))(jax.random.split(key_order, NDEV))
    return (counts, orders.astype(jnp.int32), key_tiles)


def tile_plan(key):
    counts, orders, key_tiles = route_plan(key)
    pool_size = jnp.sum(counts, axis=0)
    columns = jnp.arange(TCOLS)
    live_count = jnp.maximum((pool_size[:, None] - columns[None, :] + TCOLS - 1) // TCOLS, 0)
    places = jnp.arange(K)
    scores = jax.random.randint(key_tiles, (NDEV, TCOLS, K), 0, 2 ** 20) * K + places[None, None, :]
    scores = jnp.where(places[None, None, :] < live_count[:, :, None], scores, 2 ** 30 + places[None, None, :])
    ranked = jnp.argsort(scores, axis=-1, stable=True)
    lists = jnp.where(places[None, None, :] < live_count[:, :, None], columns[None, :, None] + TCOLS * ranked, 0)
    return (lists.astype(jnp.int32), live_count.astype(jnp.int32))


def camera_table(key):
    key = jax.random.fold_in(key, 23)
    unit_draw = jax.random.uniform(key, (VIEWS, 8), jnp.float32)
    columns = [300.0 + 300.0 * unit_draw[:, 0], -100.0 + 200.0 * unit_draw[:, 1], -20.0 + 40.0 * unit_draw[:, 2], 300.0 + 300.0 * unit_draw[:, 3], -100.0 + 200.0 * unit_draw[:, 4], -20.0 + 40.0 * unit_draw[:, 5], 0.3 + 2.5 * unit_draw[:, 6], -math.pi + 2.0 * math.pi * unit_draw[:, 7]]
    return jnp.stack(columns, axis=1)


def draw_send_index(key, part):
    counts, orders, key_tiles = route_plan(key)
    return orders.reshape(NDEV, NDEV, CAP)


def draw_send_count(key, part):
    counts, orders, key_tiles = route_plan(key)
    return counts


def draw_tile_list(key, part):
    lists, live_count = tile_plan(key)
    return lists


def draw_tile_count(key, part):
    lists, live_count = tile_plan(key)
    return live_count


def draw_cameras(key, part):
    return camera_table(key)


def draw_centers(key, part):
    counts, orders, key_tiles = route_plan(key)
    cameras = camera_table(key)
    key = jax.random.fold_in(key, 5)
    position = jnp.zeros((NDEV, G_DEV), jnp.int32).at[jnp.arange(NDEV)[:, None], orders].set(jnp.arange(G_DEV, dtype=jnp.int32)[None, :])
    target_dev = position // CAP
    slot_index = position % CAP
    taken = jnp.take_along_axis(counts, target_dev, axis=1)
    before = jnp.cumsum(counts, axis=0) - counts
    pool_item = jnp.take_along_axis(before, target_dev, axis=1) + slot_index
    home_tile = pool_item % TCOLS
    view_index = target_dev // SUB_ROWS % VIEWS
    tile_row = target_dev // (VIEWS * SUB_ROWS) * SUB_ROWS + target_dev % SUB_ROWS
    routed = slot_index < taken
    jitter = jax.random.uniform(key, (3, NDEV, G_DEV), jnp.float32)
    pixel_x = jnp.where(routed, 16.0 * home_tile + 16.0 * jitter[0] - 0.5, 16.0 * TCOLS * jitter[0])
    pixel_y = jnp.where(routed, 16.0 * tile_row + 16.0 * jitter[1] - 0.5, 16.0 * ROWS * jitter[1])
    depth_z = jitter[2]
    camera = cameras[view_index]
    world_x = (pixel_x - camera[..., 2] - camera[..., 1] * depth_z) / camera[..., 0]
    world_y = (pixel_y - camera[..., 5] - camera[..., 4] * depth_z) / camera[..., 3]
    return jnp.stack([world_x, world_y, depth_z]).reshape(3, NDEV * G_DEV)


def block_levels(stream_key, dims, shards, low, largest):
    level, own = 1.0, jax.random.fold_in(stream_key, 6)
    for dim, blocks in shards:
        heights = jnp.exp(jax.random.uniform(jax.random.fold_in(own, dim), (blocks,), jnp.float32, low / len(shards), largest / len(shards)))
        level = level * jnp.repeat(heights, dims[dim] // blocks).reshape([-1 if axis == dim else 1 for axis in range(len(dims))])
    return level


def centred(own_key, shape, scale, most, shards=(), kind=jnp.bfloat16):
    array = scale * jax.random.normal(own_key, shape, jnp.float32)
    if shards:
        array = array * block_levels(own_key, shape, shards, -0.22, 0.18)
    return jnp.clip(array, -most, most).astype(kind)


def setup_inputs(seed: int = 0, part: int = 0) -> dict:
    key_list = jax.random.split(jax.random.key(seed), 13)
    own_keys = jax.random.split(jax.random.fold_in(key_list[12], part), 13)
    centers = draw_centers(jax.random.fold_in(jax.random.fold_in(key_list[12], part), 71), part)
    scale_log = jnp.clip(-6.2 + 2.2999997 * jax.random.uniform(own_keys[1], (3, GAUSS), jnp.float32) ** block_levels(own_keys[1], (3, GAUSS), ((1, 16),), -0.2, 0.2), -6.2, -3.9)
    shear_terms = centred(own_keys[2], (3, GAUSS), 0.5, 3.0, ((1, 16),), jnp.float32)
    opacity_logit = jnp.clip(-7.0 + 5.0 * jax.random.uniform(own_keys[3], (GAUSS,), jnp.float32) ** block_levels(own_keys[3], (GAUSS,), ((0, 16),), -0.2, 0.2), -7.0, -2.0)
    sh_coeffs = centred(own_keys[4], (SH_COEF, GAUSS), 0.5, 3.0, ((1, 16),), jnp.float32)
    cameras = draw_cameras(jax.random.fold_in(jax.random.fold_in(key_list[12], part), 71), part)
    appearance = centred(own_keys[6], (VIEWS, 12), 0.2, 1.0, ((0, 2),), jnp.float32)
    target = jnp.clip(1.0 * jax.random.uniform(own_keys[7], (3, VIEWS, ROWS, TCOLS, TILE_PIX), jnp.float32) ** block_levels(own_keys[7], (3, VIEWS, ROWS, TCOLS, TILE_PIX), ((1, 2), (2, 8)), -0.2, 0.2), 0.0, 1.0)
    send_index = draw_send_index(jax.random.fold_in(jax.random.fold_in(key_list[12], part), 71), part)
    send_count = draw_send_count(jax.random.fold_in(jax.random.fold_in(key_list[12], part), 71), part)
    tile_list = draw_tile_list(jax.random.fold_in(jax.random.fold_in(key_list[12], part), 71), part)
    tile_count = draw_tile_count(jax.random.fold_in(jax.random.fold_in(key_list[12], part), 71), part)
    return {"centers": centers, "scale_log": scale_log, "shear_terms": shear_terms, "opacity_logit": opacity_logit, "sh_coeffs": sh_coeffs, "cameras": cameras, "appearance": appearance, "target": target, "send_index": send_index, "send_count": send_count, "tile_list": tile_list, "tile_count": tile_count}


HIGHEST = lax.Precision.HIGHEST

def harmonic_table(cameras):
    polar_angle = cameras[:, 6]
    azimuth = cameras[:, 7]
    unit_x = jnp.sin(polar_angle) * jnp.cos(azimuth)
    unit_y = jnp.sin(polar_angle) * jnp.sin(azimuth)
    unit_z = jnp.cos(polar_angle)
    square_x = unit_x * unit_x
    square_y = unit_y * unit_y
    square_z = unit_z * unit_z
    columns = [jnp.full_like(unit_x, 0.28209479177387814), -0.4886025119029199 * unit_y, 0.4886025119029199 * unit_z, -0.4886025119029199 * unit_x, 1.0925484305920792 * unit_x * unit_y, -1.0925484305920792 * unit_y * unit_z, 0.31539156525252005 * (2.0 * square_z - square_x - square_y), -1.0925484305920792 * unit_x * unit_z, 0.5462742152960396 * (square_x - square_y), -0.5900435899266435 * unit_y * (3.0 * square_x - square_y), 2.890611442640554 * unit_x * unit_y * unit_z, -0.4570457994644658 * unit_y * (4.0 * square_z - square_x - square_y), 0.3731763325901154 * unit_z * (2.0 * square_z - 3.0 * square_x - 3.0 * square_y), -0.4570457994644658 * unit_x * (4.0 * square_z - square_x - square_y), 1.445305721320277 * unit_z * (square_x - square_y), -0.5900435899266435 * unit_x * (square_x - 3.0 * square_y)]
    return jnp.stack(columns, axis=1)

def project(packed, camera, harmonics):
    focal_x, skew_x, center_x = (camera[0], camera[1], camera[2])
    focal_y, skew_y, center_y = (camera[3], camera[4], camera[5])
    mean_x = focal_x * packed[0] + skew_x * packed[2] + center_x
    mean_y = focal_y * packed[1] + skew_y * packed[2] + center_y
    factor_xx = jnp.exp(packed[3])
    factor_yy = jnp.exp(packed[4])
    factor_zz = jnp.exp(packed[5])
    factor_yx = packed[6] * factor_xx
    factor_zx = packed[7] * factor_xx
    factor_zy = packed[8] * factor_yy
    upper_x = focal_x * factor_xx + skew_x * factor_zx
    upper_y = skew_x * factor_zy
    upper_z = skew_x * factor_zz
    below_x = focal_y * factor_yx + skew_y * factor_zx
    below_y = focal_y * factor_yy + skew_y * factor_zy
    below_z = skew_y * factor_zz
    spread_xx = upper_x * upper_x + upper_y * upper_y + upper_z * upper_z + 0.3
    spread_xy = upper_x * below_x + upper_y * below_y + upper_z * below_z
    spread_yy = below_x * below_x + below_y * below_y + below_z * below_z + 0.3
    determinant = spread_xx * spread_yy - spread_xy * spread_xy
    opacity = jax.nn.sigmoid(packed[9])
    coeffs = packed[10:].reshape(3, 16, -1)
    colors = jnp.maximum(jnp.einsum('ckn,k->cn', coeffs, harmonics, precision=HIGHEST) + 0.5, 0.0)
    shape_rows = jnp.stack([mean_x, mean_y, spread_yy / determinant, -spread_xy / determinant, spread_xx / determinant, opacity])
    return jnp.concatenate([shape_rows, colors], axis=0)

def splat(entries, live_entry, pixel_x, pixel_y):
    delta_x = entries[0][:, :, None] - pixel_x[:, None, :]
    delta_y = entries[1][:, :, None] - pixel_y[None, None, :]
    falloff = jnp.exp(-0.5 * (entries[2][:, :, None] * delta_x * delta_x + entries[4][:, :, None] * delta_y * delta_y) - entries[3][:, :, None] * delta_x * delta_y)
    alphas = (entries[5] * live_entry)[:, :, None] * falloff
    log_keep = jnp.log1p(-alphas)
    transmit = jnp.exp(jnp.cumsum(log_keep, axis=1) - log_keep)
    return jnp.einsum('ctk,tki->cti', entries[6:9], alphas * transmit, precision=HIGHEST)

def reference(centers, scale_log, shear_terms, opacity_logit, sh_coeffs, cameras, appearance, target, send_index, send_count, tile_list, tile_count):
    packed = jnp.concatenate([centers, scale_log, shear_terms, opacity_logit[None, :], sh_coeffs], axis=0)
    harmonics = harmonic_table(cameras)
    peers = send_count.shape[0]
    tile_cols = tile_list.shape[1]
    list_len = tile_list.shape[2]
    gauss_dev = centers.shape[1] // peers
    tile_pix = target.shape[-1]
    pixel_x = (16 * jnp.arange(tile_cols)[:, None] + (jnp.arange(tile_pix) % 16)[None, :]).astype(jnp.float32)
    pixel_up = (jnp.arange(tile_pix) // 16).astype(jnp.int32)

    def one_device(source_rows, device):
        view_index = device // N_SUB % N_VIEW
        tile_row = device // (N_VIEW * N_SUB) * N_SUB + device % N_SUB
        counts = send_count[:, device]
        inclusive = jnp.cumsum(counts).astype(jnp.int32)
        entry_pool = tile_list[device].reshape(-1)
        source = lax.optimization_barrier(jnp.sum((inclusive[None, :] <= entry_pool[:, None]).astype(jnp.int32), axis=1)).astype(jnp.int32)
        slot_index = (entry_pool - (inclusive[source] - counts[source])).astype(jnp.int32)
        gauss_id = (source * gauss_dev + send_index[source, device, slot_index]).astype(jnp.int32)
        gathered = jnp.take(source_rows, gauss_id, axis=1)
        entries = project(gathered, cameras[view_index], harmonics[view_index]).reshape(9, tile_cols, list_len)
        live_entry = (jnp.arange(list_len)[None, :] < tile_count[device][:, None]).astype(jnp.float32)
        pixel_y = (16 * tile_row + pixel_up).astype(jnp.float32)
        return splat(entries, live_entry, pixel_x, pixel_y)

    def loss_fn(source_rows, correction):
        blended = lax.map(jax.checkpoint(lambda device: one_device(source_rows, device)), jnp.arange(peers, dtype=jnp.int32))
        blended = blended.reshape(N_TILE, N_VIEW, N_SUB, 3, tile_cols, tile_pix)
        blended = blended.transpose(3, 1, 0, 2, 4, 5).reshape(3, N_VIEW, N_TILE * N_SUB, tile_cols, tile_pix)
        mixing = jnp.eye(3, dtype=jnp.float32)[None] + correction[:, :9].reshape(N_VIEW, 3, 3)
        rendered = jnp.einsum('vcd,dvrti->cvrti', mixing, blended, precision=HIGHEST) + correction[:, 9:].T[:, :, None, None, None]
        loss_value = 0.5 * jnp.sum((rendered - target) ** 2)
        return (loss_value, rendered)
    loss_value, pullback, rendered = jax.vjp(loss_fn, packed, appearance, has_aux=True)
    param_grad, appear_grad = pullback(jnp.ones_like(loss_value))
    return (rendered, param_grad, appear_grad / (TILE_PIX * ROWS * TCOLS))
```

```python
import functools

import jax
import jax.numpy as jnp
from jax import lax
from jax.experimental import pallas as pl
from jax.experimental.pallas import tpu as pltpu
from jax.sharding import PartitionSpec as P

F32 = jnp.float32
BF16 = jnp.bfloat16
I32 = jnp.int32
LOG2E = 1.4426950408889634
LANES = 128
ROUTE_AXES = ("tile", "view", "sub")
NT = (((1,), (1,)), ((), ()))
PARAMS = pltpu.CompilerParams(vmem_limit_bytes=48 * 1024 * 1024)
IN_VMEM = pl.BlockSpec(memory_space=pltpu.VMEM)
IN_SMEM = pl.BlockSpec(memory_space=pltpu.SMEM)


def harmonic_table(cameras):
    polar_angle = cameras[:, 6]
    azimuth = cameras[:, 7]
    unit_x = jnp.sin(polar_angle) * jnp.cos(azimuth)
    unit_y = jnp.sin(polar_angle) * jnp.sin(azimuth)
    unit_z = jnp.cos(polar_angle)
    square_x = unit_x * unit_x
    square_y = unit_y * unit_y
    square_z = unit_z * unit_z
    columns = [
        jnp.full_like(unit_x, 0.28209479177387814),
        -0.4886025119029199 * unit_y,
        0.4886025119029199 * unit_z,
        -0.4886025119029199 * unit_x,
        1.0925484305920792 * unit_x * unit_y,
        -1.0925484305920792 * unit_y * unit_z,
        0.31539156525252005 * (2.0 * square_z - square_x - square_y),
        -1.0925484305920792 * unit_x * unit_z,
        0.5462742152960396 * (square_x - square_y),
        -0.5900435899266435 * unit_y * (3.0 * square_x - square_y),
        2.890611442640554 * unit_x * unit_y * unit_z,
        -0.4570457994644658 * unit_y * (4.0 * square_z - square_x - square_y),
        0.3731763325901154 * unit_z * (2.0 * square_z - 3.0 * square_x - 3.0 * square_y),
        -0.4570457994644658 * unit_x * (4.0 * square_z - square_x - square_y),
        1.445305721320277 * unit_z * (square_x - square_y),
        -0.5900435899266435 * unit_x * (square_x - 3.0 * square_y),
    ]
    return jnp.stack(columns, axis=0)


def project_shape(p0, p1, p2, p3, p4, p5, p6, p7, p8, camera):
    focal_x, skew_x, center_x, focal_y, skew_y, center_y = camera
    mean_x = focal_x * p0 + skew_x * p2 + center_x
    mean_y = focal_y * p1 + skew_y * p2 + center_y
    factor_xx = jnp.exp(p3)
    factor_yy = jnp.exp(p4)
    factor_zz = jnp.exp(p5)
    factor_yx = p6 * factor_xx
    factor_zx = p7 * factor_xx
    factor_zy = p8 * factor_yy
    upper_x = focal_x * factor_xx + skew_x * factor_zx
    upper_y = skew_x * factor_zy
    upper_z = skew_x * factor_zz
    below_x = focal_y * factor_yx + skew_y * factor_zx
    below_y = focal_y * factor_yy + skew_y * factor_zy
    below_z = skew_y * factor_zz
    spread_xx = upper_x * upper_x + upper_y * upper_y + upper_z * upper_z + 0.3
    spread_xy = upper_x * below_x + upper_y * below_y + upper_z * below_z
    spread_yy = below_x * below_x + below_y * below_y + below_z * below_z + 0.3
    inverse = 1.0 / (spread_xx * spread_yy - spread_xy * spread_xy)
    return (mean_x, mean_y, spread_yy * inverse, -spread_xy * inverse, spread_xx * inverse)


def lane_gather(values, lanes):
    dims = lax.GatherDimensionNumbers(
        offset_dims=(),
        collapsed_slice_dims=(1,),
        start_index_map=(1,),
        operand_batching_dims=(0,),
        start_indices_batching_dims=(0,),
    )
    return lax.gather(
        values,
        lanes[:, :, None],
        dims,
        slice_sizes=(1, 1),
        mode=lax.GatherScatterMode.PROMISE_IN_BOUNDS,
    )


def spread(row, rows):
    return jnp.broadcast_to(row, (rows, row.shape[1]))


def iota(shape, dim):
    return lax.broadcasted_iota(I32, shape, dim)


def onehot_scatter(total, high, low, first, second, live):
    blocks = total.shape[0] // 2
    hit = iota((blocks, LANES), 0) == high
    if live is not None:
        hit = jnp.logical_and(hit, live)
    left = jnp.concatenate(
        [jnp.where(hit, first, 0.0), jnp.where(hit, second, 0.0)], axis=0
    ).astype(BF16)
    right = (iota((LANES, LANES), 0) == low).astype(F32).astype(BF16)
    return total + lax.dot_general(left, right, NT, preferred_element_type=F32)


def gather_columns(out_ref, source_ref, high_ref, low_ref):
    out_blocks = high_ref.shape[0]
    blocks = source_ref.shape[1] // LANES

    def one_block(place, carry):
        high = spread(high_ref[pl.ds(place, 1), :], 8)
        low = spread(low_ref[pl.ds(place, 1), :], 8)
        found = jnp.zeros((8, LANES), F32)
        for block in range(blocks):
            cut = slice(block * LANES, (block + 1) * LANES)
            found = jnp.where(high == block, lane_gather(source_ref[0:8, cut], low), found)
        out_ref[0:8, pl.ds(pl.multiple_of(place * LANES, LANES), LANES)] = found
        return carry

    lax.fori_loop(0, out_blocks, one_block, 0)
    for group in range(out_blocks // 8):
        high = high_ref[group * 8 : group * 8 + 8, :]
        low = low_ref[group * 8 : group * 8 + 8, :]
        found = jnp.zeros((8, LANES), F32)
        for block in range(blocks):
            cut = slice(block * LANES, (block + 1) * LANES)
            row = spread(source_ref[8:9, cut], 8)
            found = jnp.where(high == block, lane_gather(row, low), found)
        for inner in range(8):
            place = group * 8 + inner
            out_ref[8:9, place * LANES : (place + 1) * LANES] = found[inner : inner + 1, :]


def select_camera(cameras_ref, view):
    chosen = []
    for column in range(6):
        value = jnp.full(view.shape, cameras_ref[0, column], F32)
        for other in range(1, cameras_ref.shape[0]):
            value = jnp.where(view == other, cameras_ref[other, column], value)
        chosen.append(value)
    return chosen


def select_harmonics(harmonics_ref, view):
    shape = (16, view.shape[1])
    value = jnp.broadcast_to(harmonics_ref[:, 0:1], shape)
    for other in range(1, harmonics_ref.shape[1]):
        value = jnp.where(
            view == other, jnp.broadcast_to(harmonics_ref[:, other : other + 1], shape), value
        )
    return value


def owner_kernel(
    sub_count,
    view_count,
    slot_cap,
    centers_ref,
    scale_ref,
    shear_ref,
    opacity_ref,
    coeff_ref,
    cameras_ref,
    harmonics_ref,
    slots_ref,
    count_ref,
    out_ref,
    place_ref,
    owner_ref,
    high_ref,
    low_ref,
    projected_ref,
):
    blocks = slots_ref.shape[0]
    slots = slots_ref[...]
    high_ref[...] = slots >> 7
    low_ref[...] = slots & 127
    peers = count_ref.shape[1]

    lane = iota((blocks, LANES), 1)

    def one_block(place, total):
        return onehot_scatter(
            total,
            high_ref[pl.ds(place, 1), :],
            low_ref[pl.ds(place, 1), :],
            place.astype(F32),
            lane.astype(F32),
            None,
        )

    table = lax.fori_loop(0, blocks, one_block, jnp.zeros((2 * blocks, LANES), F32)).astype(I32)
    place_ref[...] = table
    position = table[0:blocks] * LANES + table[blocks:]
    dest = position // slot_cap
    view = (dest // sub_count) % view_count
    within = position - dest * slot_cap
    limit = jnp.zeros_like(dest)
    for peer in range(peers):
        limit = jnp.where(dest == peer, count_ref[0, peer], limit)
    live = (within < limit).astype(I32)
    for block in range(blocks):
        cut = slice(block * LANES, (block + 1) * LANES)
        owner_ref[0:1, cut] = view[block : block + 1, :]
        owner_ref[1:2, cut] = live[block : block + 1, :]

    step = 512

    def one_chunk(number, carry):
        cut = pl.ds(pl.multiple_of(number * step, step), step)
        view_row = owner_ref[0:1, cut]
        camera = select_camera(cameras_ref, view_row)
        params = [ref[r : r + 1, cut] for ref in (centers_ref, scale_ref, shear_ref) for r in range(3)]
        rows = list(project_shape(*params, camera))
        logit = opacity_ref[0:1, cut]
        rows.append(jnp.minimum(logit, 0.0) - jnp.log1p(jnp.exp(-jnp.abs(logit))))
        basis = select_harmonics(harmonics_ref, view_row)
        for color in range(3):
            terms = coeff_ref[color * 16 : color * 16 + 16, cut] * basis
            rows.append(jnp.maximum(jnp.sum(terms, axis=0, keepdims=True) + 0.5, 0.0))
        for row in range(9):
            projected_ref[row : row + 1, cut] = rows[row]
        return carry

    lax.fori_loop(0, coeff_ref.shape[1] // step, one_chunk, 0)
    out_ref[8:16, :] = jnp.zeros((8, out_ref.shape[1]), F32)
    gather_columns(out_ref, projected_ref, high_ref, low_ref)
    for peer in range(peers):
        out_ref[9:10, peer * slot_cap : (peer + 1) * slot_cap] = jnp.full(
            (1, slot_cap), count_ref[0, peer].astype(F32)
        )


def tile_kernel(
    slot_cap,
    peers,
    sub_count,
    pool_ref,
    list_ref,
    count_ref,
    appear_ref,
    target_ref,
    out_ref,
    rendered_ref,
    entry_ref,
    alpha_ref,
    weight_ref,
    moment_ref,
    gathered_ref,
    high_ref,
    low_ref,
):
    tiles, list_len = list_ref.shape
    tile_pix = target_ref.shape[2]
    blocks = pool_ref.shape[1] // LANES
    cols = list_len // LANES
    halves = tile_pix // LANES
    tile_row = lax.axis_index("tile") * sub_count + lax.axis_index("sub")
    center_y = 16.0 * tile_row.astype(F32) + 7.5

    entries = list_ref[...]
    column = entries
    inclusive = jnp.zeros((1, LANES), I32)
    for peer in range(peers):
        start = peer * slot_cap
        received = jnp.broadcast_to(pool_ref[9:10, start : start + 1], (1, LANES)).astype(I32)
        inclusive = inclusive + received
        bound = jnp.concatenate([spread(inclusive, tiles)] * cols, axis=1)
        gap = jnp.concatenate([spread(slot_cap - received, tiles)] * cols, axis=1)
        column = column + jnp.where(bound <= entries, gap, 0)
    column = jnp.clip(column, 0, pool_ref.shape[1] - 1)
    lane = iota((tiles, list_len), 1)
    tile = iota((tiles, list_len), 0)
    live_limit = jnp.zeros((tiles, list_len), I32)
    for number in range(tiles):
        live_limit = jnp.where(tile == number, count_ref[0, number], live_limit)
    live = lane < live_limit
    high_all = column >> 7
    low_all = column & 127

    tile_x = 16.0 * iota((tiles, LANES), 0).astype(F32) + 7.5
    for col in range(cols):
        cut = slice(col * LANES, (col + 1) * LANES)
        high = high_all[:, cut]
        low = low_all[:, cut]
        found = [jnp.zeros((tiles, LANES), F32) for _ in range(9)]
        for block in range(blocks):
            hit = high == block
            for row in range(9):
                source = spread(pool_ref[row : row + 1, block * LANES : (block + 1) * LANES], tiles)
                found[row] = jnp.where(hit, lane_gather(source, low), found[row])
        found[0] = found[0] - tile_x
        found[1] = found[1] - center_y
        found[2] = found[2] * (-0.5 * LOG2E)
        found[3] = found[3] * (-LOG2E)
        found[4] = found[4] * (-0.5 * LOG2E)
        found[5] = jnp.where(live[:, cut], found[5] * LOG2E, -1e30)
        for row in range(9):
            entry_ref[row * cols + col] = found[row]

    pixel = iota((tiles, LANES), 1)
    pixel_x = (pixel & 15).astype(F32) - 7.5
    pixel_y = [((pixel + half * LANES) >> 4).astype(F32) - 7.5 for half in range(halves)]

    state = (
        tuple(jnp.ones((tiles, LANES), F32) for _ in range(halves)),
        tuple(jnp.zeros((tiles, LANES), F32) for _ in range(3 * halves)),
    )
    for col in range(cols):

        def forward(k, state, col=col):
            transmit, colors = state
            at = jnp.full((tiles, LANES), k, I32)
            row = [lane_gather(entry_ref[r * cols + col], at) for r in range(9)]
            delta_x = row[0] - pixel_x
            part = row[2] * delta_x * delta_x + row[5]
            slope = row[3] * delta_x
            new_transmit = []
            new_colors = []
            for half in range(halves):
                delta_y = row[1] - pixel_y[half]
                alpha = jnp.exp2(part + delta_y * (slope + row[4] * delta_y))
                weight = alpha * transmit[half]
                cut = slice(half * LANES, (half + 1) * LANES)
                alpha_ref[col * LANES + k, :, cut] = alpha
                weight_ref[col * LANES + k, :, cut] = weight
                new_transmit.append(transmit[half] * (1.0 - alpha))
                for color in range(3):
                    new_colors.append(colors[half * 3 + color] + weight * row[6 + color])
            return (tuple(new_transmit), tuple(new_colors))

        state = lax.fori_loop(0, LANES, forward, state, unroll=8)
    blended = [
        jnp.concatenate([state[1][half * 3 + color] for half in range(halves)], axis=1)
        for color in range(3)
    ]

    mixing = [
        [appear_ref[0, 3 * c + d] + (1.0 if c == d else 0.0) for d in range(3)] for c in range(3)
    ]
    residue = []
    for c in range(3):
        value = appear_ref[0, 9 + c]
        value = (
            mixing[c][0] * blended[0] + mixing[c][1] * blended[1] + mixing[c][2] * blended[2] + value
        )
        rendered_ref[c] = value
        residue.append(value - target_ref[c])
    back = [
        mixing[0][d] * residue[0] + mixing[1][d] * residue[1] + mixing[2][d] * residue[2]
        for d in range(3)
    ]
    sums = [residue[c] * blended[d] for c in range(3) for d in range(3)] + residue
    term_lane = iota((1, slot_cap), 1)
    term_row = jnp.zeros((1, slot_cap), F32)
    for number, values in enumerate(sums):
        total = jnp.sum(jnp.sum(values, axis=0, keepdims=True), axis=1, keepdims=True)
        term_row = jnp.where(term_lane == number, total, term_row)

    back_half = [
        [back[c][:, half * LANES : (half + 1) * LANES] for c in range(3)] for half in range(halves)
    ]
    behind = tuple(jnp.zeros((tiles, LANES), F32) for _ in range(halves))
    for col in reversed(range(cols)):

        def backward(number, behind, col=col):
            k = LANES - 1 - number
            at = jnp.full((tiles, LANES), k, I32)
            row = [lane_gather(entry_ref[r * cols + col], at) for r in (6, 7, 8)]
            new_behind = []
            for half in range(halves):
                cut = slice(half * LANES, (half + 1) * LANES)
                seen = (
                    back_half[half][0] * row[0]
                    + back_half[half][1] * row[1]
                    + back_half[half][2] * row[2]
                )
                ahead = seen - behind[half]
                alpha = alpha_ref[col * LANES + k, :, cut]
                new_behind.append(behind[half] + alpha * ahead)
                alpha_ref[col * LANES + k, :, cut] = ahead * weight_ref[col * LANES + k, :, cut]
            return tuple(new_behind)

        behind = lax.fori_loop(0, LANES, backward, behind, unroll=8)

    pix = iota((16, tile_pix), 1)
    mono_x = (pix & 15).astype(F32) - 7.5
    mono_y = (pix >> 4).astype(F32) - 7.5
    kind = iota((16, tile_pix), 0)
    mono = jnp.where(kind == 0, 1.0, 0.0)
    for number, values in enumerate(
        (mono_x, mono_y, mono_x * mono_x, mono_x * mono_y, mono_y * mono_y)
    ):
        mono = jnp.where(kind == number + 1, values, mono)
    mono = mono.astype(BF16)
    back_all = jnp.concatenate(back, axis=0)
    back_high = back_all.astype(BF16)
    back_low = (back_all - back_high.astype(F32)).astype(BF16)
    back_both = jnp.concatenate([back_high, back_low], axis=0)
    steps = 32
    width = steps * tiles
    own_tile = iota((tiles, width), 0) == (iota((tiles, width), 1) & (tiles - 1))

    def reduce_pixels(number, carry):
        cut = pl.ds(pl.multiple_of(number * width, width), width)
        power = alpha_ref[pl.ds(number * steps, steps)].reshape(width, tile_pix)
        power_high = power.astype(BF16)
        power_low = (power - power_high.astype(F32)).astype(BF16)
        moments = lax.dot_general(mono, power_high, NT, preferred_element_type=F32)
        moments = moments + lax.dot_general(mono, power_low, NT, preferred_element_type=F32)
        moment_ref[0:8, cut] = moments[0:8]
        weight = weight_ref[pl.ds(number * steps, steps)].reshape(width, tile_pix)
        weight_high = weight.astype(BF16)
        weight_low = (weight - weight_high.astype(F32)).astype(BF16)
        colors = lax.dot_general(back_both, weight_high, NT, preferred_element_type=F32)
        colors = colors[: 3 * tiles] + colors[3 * tiles :]
        colors = colors + lax.dot_general(back_high, weight_low, NT, preferred_element_type=F32)
        for color in range(3):
            own = jnp.where(own_tile, colors[color * tiles : (color + 1) * tiles], 0.0)
            moment_ref[6 + color : 7 + color, cut] = jnp.sum(own, axis=0, keepdims=True)
        return carry

    lax.fori_loop(0, list_len // steps, reduce_pixels, 0)

    table = jnp.zeros((2 * blocks, LANES), F32)
    place_lane = iota((1, LANES), 1)
    for number in range(tiles):
        for col in range(cols):
            cut = slice(col * LANES, (col + 1) * LANES)
            k = place_lane + col * LANES
            flat = k * tiles + number
            table = onehot_scatter(
                table,
                high_all[number : number + 1, cut],
                low_all[number : number + 1, cut],
                (flat >> 7).astype(F32),
                (flat & 127).astype(F32),
                k < count_ref[0, number],
            )
    table = table.astype(I32)
    high_ref[...] = table[0:blocks]
    low_ref[...] = table[blocks:]
    gather_columns(gathered_ref, moment_ref, high_ref, low_ref)

    for block in range(blocks):
        cut = slice(block * LANES, (block + 1) * LANES)
        own = (table[blocks + block : blocks + block + 1, :] & (tiles - 1)).astype(F32)
        local_x = pool_ref[0:1, cut] - (16.0 * own + 7.5)
        local_y = pool_ref[1:2, cut] - center_y
        conic_a = pool_ref[2:3, cut]
        conic_b = pool_ref[3:4, cut]
        conic_c = pool_ref[4:5, cut]
        one, m_x, m_y, m_xx, m_xy, m_yy = [gathered_ref[r : r + 1, cut] for r in range(6)]
        d_x = local_x * one - m_x
        d_y = local_y * one - m_y
        d_xx = local_x * d_x - (local_x * m_x - m_xx)
        d_xy = local_y * d_x - (local_x * m_y - m_xy)
        d_yy = local_y * d_y - (local_y * m_y - m_yy)
        out_ref[0:1, cut] = -(conic_a * d_x + conic_b * d_y)
        out_ref[1:2, cut] = -(conic_c * d_y + conic_b * d_x)
        out_ref[2:3, cut] = -0.5 * d_xx
        out_ref[3:4, cut] = -d_xy
        out_ref[4:5, cut] = -0.5 * d_yy
        out_ref[5:6, cut] = one
    out_ref[6:8, :] = gathered_ref[6:8, :]
    out_ref[8:16, :] = jnp.zeros((8, out_ref.shape[1]), F32)
    out_ref[8:9, :] = gathered_ref[8:9, :]
    for peer in range(peers):
        out_ref[9:10, peer * slot_cap : (peer + 1) * slot_cap] = term_row


def gradient_kernel(
    sub_count,
    view_count,
    slot_cap,
    peers,
    pixels,
    centers_ref,
    scale_ref,
    shear_ref,
    opacity_ref,
    coeff_ref,
    cameras_ref,
    harmonics_ref,
    place_ref,
    owner_ref,
    back_ref,
    out_ref,
    appear_ref,
    gathered_ref,
    high_ref,
    low_ref,
):
    blocks = high_ref.shape[0]
    high_ref[...] = place_ref[0:blocks, :]
    low_ref[...] = place_ref[blocks:, :]
    gather_columns(gathered_ref, back_ref, high_ref, low_ref)
    step = 512

    def one_chunk(number, carry):
        cut = pl.ds(pl.multiple_of(number * step, step), step)
        view_row = owner_ref[0:1, cut]
        live = owner_ref[1:2, cut] > 0
        grads = [jnp.where(live, gathered_ref[r : r + 1, cut], 0.0) for r in range(9)]
        camera = select_camera(cameras_ref, view_row)
        params = [ref[r : r + 1, cut] for ref in (centers_ref, scale_ref, shear_ref) for r in range(3)]
        _, pullback = jax.vjp(lambda *rows: project_shape(*rows, camera), *params)
        for row, value in enumerate(pullback(tuple(grads[:5]))):
            out_ref[row : row + 1, cut] = value
        out_ref[9:10, cut] = grads[5] / (1.0 + jnp.exp(opacity_ref[0:1, cut]))
        basis = select_harmonics(harmonics_ref, view_row)
        for color in range(3):
            terms = coeff_ref[color * 16 : color * 16 + 16, cut] * basis
            value = jnp.sum(terms, axis=0, keepdims=True) + 0.5
            slope = jnp.where(value > 0.0, 1.0, jnp.where(value == 0.0, 0.5, 0.0))
            out_ref[10 + 16 * color : 26 + 16 * color, cut] = basis * (slope * grads[6 + color])
        return carry

    lax.fori_loop(0, coeff_ref.shape[1] // step, one_chunk, 0)
    mine = lax.axis_index("view")
    total = jnp.zeros((1, slot_cap), F32)
    for peer in range(peers):
        same = ((peer // sub_count) % view_count == mine).astype(F32)
        total = total + same * back_ref[9:10, peer * slot_cap : (peer + 1) * slot_cap]
    appear_ref[...] = (total * (1.0 / pixels))[:, :12]


def exchange(rows):
    return lax.all_to_all(rows, ROUTE_AXES, split_axis=1, concat_axis=1, tiled=True)


def on_device(
    centers,
    scale_log,
    shear_terms,
    opacity_logit,
    sh_coeffs,
    cameras,
    appearance,
    target,
    send_index,
    send_count,
    tile_list,
    tile_count,
):
    peers, slot_cap = send_index.shape[1:]
    slots = peers * slot_cap
    blocks = slots // LANES
    gauss_count = centers.shape[1]
    tiles, list_len = tile_list.shape[1:]
    tile_pix = target.shape[-1]
    sub_count = lax.axis_size("sub")
    view_count = lax.axis_size("view")
    tile_devs = lax.axis_size("tile")
    harmonics = harmonic_table(cameras)
    opacity_row = opacity_logit[None, :]
    source = (centers, scale_log, shear_terms, opacity_row, sh_coeffs, cameras, harmonics)
    source_specs = [IN_VMEM] * 5 + [IN_SMEM, IN_VMEM]
    outgoing, place, owner = pl.pallas_call(
        functools.partial(owner_kernel, sub_count, view_count, slot_cap),
        out_shape=(
            jax.ShapeDtypeStruct((16, slots), F32),
            jax.ShapeDtypeStruct((2 * blocks, LANES), I32),
            jax.ShapeDtypeStruct((8, gauss_count), I32),
        ),
        in_specs=source_specs + [IN_VMEM, IN_SMEM],
        out_specs=(IN_VMEM,) * 3,
        scratch_shapes=[
            pltpu.VMEM((blocks, LANES), I32),
            pltpu.VMEM((blocks, LANES), I32),
            pltpu.VMEM((16, gauss_count), F32),
        ],
        compiler_params=PARAMS,
        name="owner_rows",
    )(*source, send_index.reshape(blocks, LANES), send_count)
    arrived = exchange(outgoing)
    returning, rendered = pl.pallas_call(
        functools.partial(tile_kernel, slot_cap, peers, sub_count),
        out_shape=(
            jax.ShapeDtypeStruct((16, slots), F32),
            jax.ShapeDtypeStruct((3, tiles, tile_pix), F32),
        ),
        in_specs=[IN_VMEM, IN_VMEM, IN_SMEM, IN_SMEM, IN_VMEM],
        out_specs=(IN_VMEM,) * 2,
        scratch_shapes=[
            pltpu.VMEM((9 * list_len // LANES, tiles, LANES), F32),
            pltpu.VMEM((list_len, tiles, tile_pix), F32),
            pltpu.VMEM((list_len, tiles, tile_pix), F32),
            pltpu.VMEM((16, tiles * list_len), F32),
            pltpu.VMEM((16, slots), F32),
            pltpu.VMEM((blocks, LANES), I32),
            pltpu.VMEM((blocks, LANES), I32),
        ],
        compiler_params=PARAMS,
        name="tile_blend",
    )(arrived, tile_list[0], tile_count, appearance, target[:, 0, 0])
    returned = exchange(returning)
    param_grad, appearance_grad = pl.pallas_call(
        functools.partial(
            gradient_kernel,
            sub_count,
            view_count,
            slot_cap,
            peers,
            float(tile_devs * sub_count * tiles * tile_pix),
        ),
        out_shape=(
            jax.ShapeDtypeStruct((10 + sh_coeffs.shape[0], gauss_count), F32),
            jax.ShapeDtypeStruct((1, 12), F32),
        ),
        in_specs=source_specs + [IN_VMEM] * 3,
        out_specs=(IN_VMEM,) * 2,
        scratch_shapes=[
            pltpu.VMEM((16, gauss_count), F32),
            pltpu.VMEM((blocks, LANES), I32),
            pltpu.VMEM((blocks, LANES), I32),
        ],
        compiler_params=PARAMS,
        name="owner_gradient",
    )(*source, place, owner, returned)
    return (rendered[:, None, None], param_grad, appearance_grad)


def solution(mesh):
    return jax.shard_map(
        on_device,
        mesh=mesh,
        in_specs=(
            P(None, ("group", "tile", "view", "sub")),
            P(None, ("group", "tile", "view", "sub")),
            P(None, ("group", "tile", "view", "sub")),
            P(("group", "tile", "view", "sub")),
            P(None, ("group", "tile", "view", "sub")),
            P("group", None),
            P(("group", "view"), None),
            P(None, ("group", "view"), ("tile", "sub"), None, None),
            P(("group", "tile", "view", "sub"), None, None),
            P(("group", "tile", "view", "sub"), None),
            P(("group", "tile", "view", "sub"), None, None),
            P(("group", "tile", "view", "sub"), None),
        ),
        out_specs=(
            P(None, ("group", "view"), ("tile", "sub"), None, None),
            P(None, ("group", "tile", "view", "sub")),
            P(("group", "view"), None),
        ),
        check_vma=False,
    )
```

```python
import functools

import jax
import jax.numpy as jnp
from jax import lax
from jax.experimental import pallas as pl
from jax.experimental.pallas import tpu as pltpu
from jax.sharding import PartitionSpec as P

F32 = jnp.float32
BF16 = jnp.bfloat16
I32 = jnp.int32
LOG2E = 1.4426950408889634
LANES = 128
ROUTE_AXES = ("tile", "view", "sub")
NT = (((1,), (1,)), ((), ()))
PARAMS = pltpu.CompilerParams(vmem_limit_bytes=48 * 1024 * 1024)
IN_VMEM = pl.BlockSpec(memory_space=pltpu.VMEM)
IN_SMEM = pl.BlockSpec(memory_space=pltpu.SMEM)


def harmonic_table(cameras):
    polar_angle = cameras[:, 6]
    azimuth = cameras[:, 7]
    unit_x = jnp.sin(polar_angle) * jnp.cos(azimuth)
    unit_y = jnp.sin(polar_angle) * jnp.sin(azimuth)
    unit_z = jnp.cos(polar_angle)
    square_x = unit_x * unit_x
    square_y = unit_y * unit_y
    square_z = unit_z * unit_z
    columns = [
        jnp.full_like(unit_x, 0.28209479177387814),
        -0.4886025119029199 * unit_y,
        0.4886025119029199 * unit_z,
        -0.4886025119029199 * unit_x,
        1.0925484305920792 * unit_x * unit_y,
        -1.0925484305920792 * unit_y * unit_z,
        0.31539156525252005 * (2.0 * square_z - square_x - square_y),
        -1.0925484305920792 * unit_x * unit_z,
        0.5462742152960396 * (square_x - square_y),
        -0.5900435899266435 * unit_y * (3.0 * square_x - square_y),
        2.890611442640554 * unit_x * unit_y * unit_z,
        -0.4570457994644658 * unit_y * (4.0 * square_z - square_x - square_y),
        0.3731763325901154 * unit_z * (2.0 * square_z - 3.0 * square_x - 3.0 * square_y),
        -0.4570457994644658 * unit_x * (4.0 * square_z - square_x - square_y),
        1.445305721320277 * unit_z * (square_x - square_y),
        -0.5900435899266435 * unit_x * (square_x - 3.0 * square_y),
    ]
    return jnp.stack(columns, axis=0)


def project_shape(p0, p1, p2, p3, p4, p5, p6, p7, p8, camera):
    focal_x, skew_x, center_x, focal_y, skew_y, center_y = camera
    mean_x = focal_x * p0 + skew_x * p2 + center_x
    mean_y = focal_y * p1 + skew_y * p2 + center_y
    factor_xx = jnp.exp(p3)
    factor_yy = jnp.exp(p4)
    factor_zz = jnp.exp(p5)
    factor_yx = p6 * factor_xx
    factor_zx = p7 * factor_xx
    factor_zy = p8 * factor_yy
    upper_x = focal_x * factor_xx + skew_x * factor_zx
    upper_y = skew_x * factor_zy
    upper_z = skew_x * factor_zz
    below_x = focal_y * factor_yx + skew_y * factor_zx
    below_y = focal_y * factor_yy + skew_y * factor_zy
    below_z = skew_y * factor_zz
    spread_xx = upper_x * upper_x + upper_y * upper_y + upper_z * upper_z + 0.3
    spread_xy = upper_x * below_x + upper_y * below_y + upper_z * below_z
    spread_yy = below_x * below_x + below_y * below_y + below_z * below_z + 0.3
    inverse = 1.0 / (spread_xx * spread_yy - spread_xy * spread_xy)
    return (mean_x, mean_y, spread_yy * inverse, -spread_xy * inverse, spread_xx * inverse)


def lane_gather(values, lanes):
    dims = lax.GatherDimensionNumbers(
        offset_dims=(),
        collapsed_slice_dims=(1,),
        start_index_map=(1,),
        operand_batching_dims=(0,),
        start_indices_batching_dims=(0,),
    )
    return lax.gather(
        values,
        lanes[:, :, None],
        dims,
        slice_sizes=(1, 1),
        mode=lax.GatherScatterMode.PROMISE_IN_BOUNDS,
    )


def spread(row, rows):
    return jnp.broadcast_to(row, (rows, row.shape[1]))


def iota(shape, dim):
    return lax.broadcasted_iota(I32, shape, dim)


def divide(values, number):
    if number & (number - 1) == 0:
        return values >> (number.bit_length() - 1)
    return lax.div(values, jnp.full_like(values, number))


def inverse_table(blocks, items):
    total = jnp.zeros((2 * blocks, LANES), F32)
    group = 8
    for start in range(0, len(items), group):
        lefts, rights = [], []
        for high, low, first, second, live in items[start : start + group]:
            hit = iota((blocks, LANES), 0) == high
            if live is not None:
                hit = jnp.logical_and(hit, live)
            lefts.append(
                jnp.concatenate([jnp.where(hit, first, 0.0), jnp.where(hit, second, 0.0)], axis=0)
            )
            rights.append((iota((LANES, LANES), 0) == low).astype(F32))
        left = jnp.concatenate(lefts, axis=1).astype(BF16)
        right = jnp.concatenate(rights, axis=1).astype(BF16)
        total = total + lax.dot_general(left, right, NT, preferred_element_type=F32)
    return total.astype(I32)


def gather_columns(high_ref, low_ref, blocks, tile_of, ninth_of, finish, finish_ninth):
    places = high_ref.shape[0]
    together = 4
    for group in range(places // 8):
        high = high_ref[group * 8 : group * 8 + 8, :]
        low = low_ref[group * 8 : group * 8 + 8, :]
        found = jnp.zeros((8, LANES), F32)
        for block in range(blocks):
            found = jnp.where(high == block, lane_gather(spread(ninth_of(block), 8), low), found)
        for inner in range(8):
            finish_ninth(group * 8 + inner, found[inner : inner + 1, :])

    def some_blocks(number, carry):
        first = number * together
        high = [spread(high_ref[pl.ds(first + n, 1), :], 8) for n in range(together)]
        low = [spread(low_ref[pl.ds(first + n, 1), :], 8) for n in range(together)]
        found = [jnp.zeros((8, LANES), F32) for _ in range(together)]
        for block in range(blocks):
            values = tile_of(block)
            for n in range(together):
                found[n] = jnp.where(high[n] == block, lane_gather(values, low[n]), found[n])
        for n in range(together):
            finish(first + n, found[n], low[n])
        return carry

    lax.fori_loop(0, places // together, some_blocks, 0)


class Packet:
    def __init__(self, ref, slot_cap):
        self.ref = ref
        self.cap = slot_cap
        self.deep = max(slot_cap // LANES, 1)

    def tile(self, block):
        start = (block % self.deep) * 8
        if not isinstance(block, int):
            start = pl.multiple_of(start, 8)
        return (block // self.deep, pl.ds(start, 8), slice(None))

    def row(self, block, number):
        start = (block % self.deep) * 8 + number if number < 8 else self.deep * 8 + block % self.deep
        return (block // self.deep, slice(start, start + 1), slice(None))

    def extra(self, peer):
        start = peer * self.cap
        lanes = slice(start % LANES, start % LANES + min(self.cap, LANES))
        return (start // LANES // self.deep, slice(9 * self.deep, 9 * self.deep + 1), lanes)


def select_camera(cameras_ref, view):
    chosen = []
    for column in range(6):
        value = jnp.full(view.shape, cameras_ref[0, column], F32)
        for other in range(1, cameras_ref.shape[0]):
            value = jnp.where(view == other, cameras_ref[other, column], value)
        chosen.append(value)
    return chosen


def select_harmonics(harmonics_ref, view):
    shape = (16, view.shape[1])
    value = jnp.broadcast_to(harmonics_ref[:, 0:1], shape)
    for other in range(1, harmonics_ref.shape[1]):
        value = jnp.where(
            view == other, jnp.broadcast_to(harmonics_ref[:, other : other + 1], shape), value
        )
    return value


def owner_kernel(
    sub_count,
    view_count,
    slot_cap,
    centers_ref,
    scale_ref,
    shear_ref,
    opacity_ref,
    coeff_ref,
    cameras_ref,
    harmonics_ref,
    slots_ref,
    count_ref,
    out_ref,
    place_ref,
    owner_ref,
    high_ref,
    low_ref,
    projected_ref,
):
    blocks = high_ref.shape[0]
    wide = slots_ref.shape[1] // LANES
    peers = count_ref.shape[1]
    packet = Packet(out_ref, slot_cap)
    lane = iota((1, LANES), 1).astype(F32)
    items = []
    for block in range(blocks):
        cut = slice((block % wide) * LANES, (block % wide + 1) * LANES)
        row = slots_ref[block // wide : block // wide + 1, cut]
        high = row >> 7
        low = row & 127
        high_ref[block : block + 1, :] = high
        low_ref[block : block + 1, :] = low
        items.append((high, low, float(block), lane, None))
    table = inverse_table(blocks, items)
    place_ref[...] = table
    position = table[0:blocks] * LANES + table[blocks:]
    dest = divide(position, slot_cap)
    view = lax.rem(divide(dest, sub_count), jnp.full_like(dest, view_count))
    within = position - dest * slot_cap
    limit = jnp.zeros_like(dest)
    for peer in range(peers):
        limit = jnp.where(dest == peer, count_ref[0, peer], limit)
    live = (within < limit).astype(F32)
    view = view.astype(F32)
    for block in range(blocks):
        cut = slice(block * LANES, (block + 1) * LANES)
        owner_ref[0:1, cut] = view[block : block + 1, :]
        owner_ref[1:2, cut] = live[block : block + 1, :]

    step = 512

    def one_chunk(number, carry):
        cut = pl.ds(pl.multiple_of(number * step, step), step)
        view_row = owner_ref[0:1, cut]
        camera = select_camera(cameras_ref, view_row)
        params = [ref[r : r + 1, cut] for ref in (centers_ref, scale_ref, shear_ref) for r in range(3)]
        rows = list(project_shape(*params, camera))
        logit = opacity_ref[0:1, cut]
        rows.append(jnp.minimum(logit, 0.0) - jnp.log1p(jnp.exp(-jnp.abs(logit))))
        basis = select_harmonics(harmonics_ref, view_row)
        for color in range(3):
            terms = coeff_ref[color * 16 : color * 16 + 16, cut] * basis
            value = jnp.sum(terms, axis=0, keepdims=True) + 0.5
            slope = jnp.where(value > 0.0, 1.0, jnp.where(value == 0.0, 0.5, 0.0))
            owner_ref[2 + color : 3 + color, cut] = slope
            rows.append(jnp.maximum(value, 0.0))
        for row in range(9):
            projected_ref[row : row + 1, cut] = rows[row]
        return carry

    lax.fori_loop(0, coeff_ref.shape[1] // step, one_chunk, 0)

    def tile_of(block):
        return projected_ref[0:8, block * LANES : (block + 1) * LANES]

    def ninth_of(block):
        return projected_ref[8:9, block * LANES : (block + 1) * LANES]

    def finish(place, found, low):
        out_ref[packet.tile(place)] = found

    def finish_ninth(place, found):
        out_ref[packet.row(place, 8)] = found

    gather_columns(
        high_ref, low_ref, projected_ref.shape[1] // LANES, tile_of, ninth_of, finish, finish_ninth
    )
    for peer in range(peers):
        out_ref[packet.extra(peer)] = jnp.full(
            (1, min(slot_cap, LANES)), count_ref[0, peer].astype(F32)
        )


def tile_kernel(
    slot_cap,
    peers,
    sub_count,
    pool_ref,
    list_ref,
    count_ref,
    appear_ref,
    target_ref,
    out_ref,
    rendered_ref,
    entry_ref,
    alpha_ref,
    weight_ref,
    moment_ref,
    high_ref,
    low_ref,
):
    tiles, list_len = list_ref.shape
    tile_pix = target_ref.shape[2]
    blocks = high_ref.shape[0]
    pool = Packet(pool_ref, slot_cap)
    packet = Packet(out_ref, slot_cap)
    cols = list_len // LANES
    halves = tile_pix // LANES
    tile_row = lax.axis_index("tile") * sub_count + lax.axis_index("sub")
    center_y = 16.0 * tile_row.astype(F32) + 7.5

    entries = list_ref[...]
    column = entries
    inclusive = jnp.zeros((1, LANES), I32)
    for peer in range(peers):
        received = pool_ref[pool.extra(peer)]
        if slot_cap < LANES:
            received = jnp.broadcast_to(received[:, 0:1], (1, LANES))
        received = received.astype(I32)
        inclusive = inclusive + received
        bound = jnp.concatenate([spread(inclusive, tiles)] * cols, axis=1)
        gap = jnp.concatenate([spread(slot_cap - received, tiles)] * cols, axis=1)
        column = column + jnp.where(bound <= entries, gap, 0)
    column = jnp.clip(column, 0, blocks * LANES - 1)
    lane = iota((tiles, list_len), 1)
    tile = iota((tiles, list_len), 0)
    live_limit = jnp.zeros((tiles, list_len), I32)
    for number in range(tiles):
        live_limit = jnp.where(tile == number, count_ref[0, number], live_limit)
    live = lane < live_limit
    high_all = column >> 7
    low_all = column & 127

    tile_x = 16.0 * iota((tiles, LANES), 0).astype(F32) + 7.5
    for col in range(cols):
        cut = slice(col * LANES, (col + 1) * LANES)
        high = high_all[:, cut]
        low = low_all[:, cut]
        found = [jnp.zeros((tiles, LANES), F32) for _ in range(9)]
        for block in range(blocks):
            hit = high == block
            for row in range(9):
                source = spread(pool_ref[pool.row(block, row)], tiles)
                found[row] = jnp.where(hit, lane_gather(source, low), found[row])
        found[0] = found[0] - tile_x
        found[1] = found[1] - center_y
        found[2] = found[2] * (-0.5 * LOG2E)
        found[3] = found[3] * (-LOG2E)
        found[4] = found[4] * (-0.5 * LOG2E)
        found[5] = jnp.where(live[:, cut], found[5] * LOG2E, -1e30)
        for row in range(9):
            entry_ref[row * cols + col] = found[row]

    pixel = iota((tiles, LANES), 1)
    pixel_x = (pixel & 15).astype(F32) - 7.5
    pixel_y = [((pixel + half * LANES) >> 4).astype(F32) - 7.5 for half in range(halves)]

    state = (
        tuple(jnp.ones((tiles, LANES), F32) for _ in range(halves)),
        tuple(jnp.zeros((tiles, LANES), F32) for _ in range(3 * halves)),
    )
    for col in range(cols):

        def forward(k, state, col=col):
            transmit, colors = state
            at = jnp.full((tiles, LANES), k, I32)
            row = [lane_gather(entry_ref[r * cols + col], at) for r in range(9)]
            delta_x = row[0] - pixel_x
            part = row[2] * delta_x * delta_x + row[5]
            slope = row[3] * delta_x
            new_transmit = []
            new_colors = []
            for half in range(halves):
                delta_y = row[1] - pixel_y[half]
                alpha = jnp.exp2(part + delta_y * (slope + row[4] * delta_y))
                weight = alpha * transmit[half]
                cut = slice(half * LANES, (half + 1) * LANES)
                alpha_ref[col * LANES + k, :, cut] = alpha
                weight_ref[col * LANES + k, :, cut] = weight
                new_transmit.append(transmit[half] * (1.0 - alpha))
                for color in range(3):
                    new_colors.append(colors[half * 3 + color] + weight * row[6 + color])
            return (tuple(new_transmit), tuple(new_colors))

        state = lax.fori_loop(0, LANES, forward, state, unroll=8)
    blended = [
        jnp.concatenate([state[1][half * 3 + color] for half in range(halves)], axis=1)
        for color in range(3)
    ]

    mixing = [
        [appear_ref[0, 3 * c + d] + (1.0 if c == d else 0.0) for d in range(3)] for c in range(3)
    ]
    residue = []
    for c in range(3):
        value = appear_ref[0, 9 + c]
        value = (
            mixing[c][0] * blended[0] + mixing[c][1] * blended[1] + mixing[c][2] * blended[2] + value
        )
        rendered_ref[c] = value
        residue.append(value - target_ref[c])
    back = [
        mixing[0][d] * residue[0] + mixing[1][d] * residue[1] + mixing[2][d] * residue[2]
        for d in range(3)
    ]
    sums = [residue[c] * blended[d] for c in range(3) for d in range(3)] + residue
    term_lane = iota((1, min(slot_cap, LANES)), 1)
    term_row = jnp.zeros((1, min(slot_cap, LANES)), F32)
    for number, values in enumerate(sums):
        total = jnp.sum(jnp.sum(values, axis=0, keepdims=True), axis=1, keepdims=True)
        term_row = jnp.where(term_lane == number, total, term_row)

    back_half = [
        [back[c][:, half * LANES : (half + 1) * LANES] for c in range(3)] for half in range(halves)
    ]
    behind = tuple(jnp.zeros((tiles, LANES), F32) for _ in range(halves))
    for col in reversed(range(cols)):

        def backward(number, behind, col=col):
            k = LANES - 1 - number
            at = jnp.full((tiles, LANES), k, I32)
            row = [lane_gather(entry_ref[r * cols + col], at) for r in (6, 7, 8)]
            new_behind = []
            for half in range(halves):
                cut = slice(half * LANES, (half + 1) * LANES)
                seen = (
                    back_half[half][0] * row[0]
                    + back_half[half][1] * row[1]
                    + back_half[half][2] * row[2]
                )
                ahead = seen - behind[half]
                alpha = alpha_ref[col * LANES + k, :, cut]
                new_behind.append(behind[half] + alpha * ahead)
                alpha_ref[col * LANES + k, :, cut] = ahead * weight_ref[col * LANES + k, :, cut]
            return tuple(new_behind)

        behind = lax.fori_loop(0, LANES, backward, behind, unroll=8)

    pix = iota((16, tile_pix), 1)
    mono_x = (pix & 15).astype(F32) - 7.5
    mono_y = (pix >> 4).astype(F32) - 7.5
    kind = iota((16, tile_pix), 0)
    mono = jnp.where(kind == 0, 1.0, 0.0)
    for number, values in enumerate(
        (mono_x, mono_y, mono_x * mono_x, mono_x * mono_y, mono_y * mono_y)
    ):
        mono = jnp.where(kind == number + 1, values, mono)
    mono = mono.astype(BF16)
    back_all = jnp.concatenate(back, axis=0)
    back_high = back_all.astype(BF16)
    back_low = (back_all - back_high.astype(F32)).astype(BF16)
    back_both = jnp.concatenate([back_high, back_low], axis=0)
    steps = 32
    width = steps * tiles
    own_tile = iota((tiles, width), 0) == (iota((tiles, width), 1) & (tiles - 1))

    def reduce_pixels(number, carry):
        cut = pl.ds(pl.multiple_of(number * width, width), width)
        power = alpha_ref[pl.ds(number * steps, steps)].reshape(width, tile_pix)
        power_high = power.astype(BF16)
        power_low = (power - power_high.astype(F32)).astype(BF16)
        moments = lax.dot_general(mono, power_high, NT, preferred_element_type=F32)
        moments = moments + lax.dot_general(mono, power_low, NT, preferred_element_type=F32)
        moment_ref[0:8, cut] = moments[0:8]
        weight = weight_ref[pl.ds(number * steps, steps)].reshape(width, tile_pix)
        weight_high = weight.astype(BF16)
        weight_low = (weight - weight_high.astype(F32)).astype(BF16)
        colors = lax.dot_general(back_both, weight_high, NT, preferred_element_type=F32)
        colors = colors[: 3 * tiles] + colors[3 * tiles :]
        colors = colors + lax.dot_general(back_high, weight_low, NT, preferred_element_type=F32)
        for color in range(3):
            own = jnp.where(own_tile, colors[color * tiles : (color + 1) * tiles], 0.0)
            moment_ref[6 + color : 7 + color, cut] = jnp.sum(own, axis=0, keepdims=True)
        return carry

    lax.fori_loop(0, list_len // steps, reduce_pixels, 0)

    items = []
    place_lane = iota((1, LANES), 1)
    for number in range(tiles):
        for col in range(cols):
            cut = slice(col * LANES, (col + 1) * LANES)
            k = place_lane + col * LANES
            flat = k * tiles + number
            items.append(
                (
                    high_all[number : number + 1, cut],
                    low_all[number : number + 1, cut],
                    (flat >> 7).astype(F32),
                    (flat & 127).astype(F32),
                    k < count_ref[0, number],
                )
            )
    table = inverse_table(blocks, items)
    high_ref[...] = table[0:blocks]
    low_ref[...] = table[blocks:]

    def tile_of(block):
        return moment_ref[0:8, block * LANES : (block + 1) * LANES]

    def ninth_of(block):
        return moment_ref[8:9, block * LANES : (block + 1) * LANES]

    def finish(place, found, low):
        at = packet.tile(place)
        own = (low[0:1] & (tiles - 1)).astype(F32)
        shape = pool_ref[at]
        local_x = shape[0:1] - (16.0 * own + 7.5)
        local_y = shape[1:2] - center_y
        conic_a, conic_b, conic_c = shape[2:3], shape[3:4], shape[4:5]
        one, m_x, m_y, m_xx, m_xy, m_yy = [found[r : r + 1] for r in range(6)]
        d_x = local_x * one - m_x
        d_y = local_y * one - m_y
        d_xx = local_x * d_x - (local_x * m_x - m_xx)
        d_xy = local_y * d_x - (local_x * m_y - m_xy)
        d_yy = local_y * d_y - (local_y * m_y - m_yy)
        out_ref[at] = jnp.concatenate(
            [
                -(conic_a * d_x + conic_b * d_y),
                -(conic_c * d_y + conic_b * d_x),
                -0.5 * d_xx,
                -d_xy,
                -0.5 * d_yy,
                one,
                found[6:8],
            ],
            axis=0,
        )

    def finish_ninth(place, found):
        out_ref[packet.row(place, 8)] = found

    gather_columns(
        high_ref, low_ref, moment_ref.shape[1] // LANES, tile_of, ninth_of, finish, finish_ninth
    )
    for peer in range(peers):
        out_ref[packet.extra(peer)] = term_row


def gradient_kernel(
    sub_count,
    view_count,
    slot_cap,
    peers,
    pixels,
    centers_ref,
    scale_ref,
    shear_ref,
    opacity_ref,
    cameras_ref,
    harmonics_ref,
    place_ref,
    owner_ref,
    back_ref,
    out_ref,
    appear_ref,
    gathered_ref,
    high_ref,
    low_ref,
):
    blocks = high_ref.shape[0]
    packet = Packet(back_ref, slot_cap)
    high_ref[...] = place_ref[0:blocks, :]
    low_ref[...] = place_ref[blocks:, :]

    def tile_of(block):
        return back_ref[packet.tile(block)]

    def ninth_of(block):
        return back_ref[packet.row(block, 8)]

    def finish(place, found, low):
        gathered_ref[0:8, pl.ds(pl.multiple_of(place * LANES, LANES), LANES)] = found

    def finish_ninth(place, found):
        gathered_ref[8:9, place * LANES : (place + 1) * LANES] = found

    gather_columns(high_ref, low_ref, blocks, tile_of, ninth_of, finish, finish_ninth)
    step = 512

    def one_chunk(number, carry):
        cut = pl.ds(pl.multiple_of(number * step, step), step)
        view_row = owner_ref[0:1, cut]
        live = owner_ref[1:2, cut] > 0.0
        grads = [jnp.where(live, gathered_ref[r : r + 1, cut], 0.0) for r in range(9)]
        camera = select_camera(cameras_ref, view_row)
        params = [ref[r : r + 1, cut] for ref in (centers_ref, scale_ref, shear_ref) for r in range(3)]
        _, pullback = jax.vjp(lambda *rows: project_shape(*rows, camera), *params)
        for row, value in enumerate(pullback(tuple(grads[:5]))):
            out_ref[row : row + 1, cut] = value
        out_ref[9:10, cut] = grads[5] / (1.0 + jnp.exp(opacity_ref[0:1, cut]))
        basis = select_harmonics(harmonics_ref, view_row)
        for color in range(3):
            slope = owner_ref[2 + color : 3 + color, cut]
            out_ref[10 + 16 * color : 26 + 16 * color, cut] = basis * (slope * grads[6 + color])
        return carry

    lax.fori_loop(0, out_ref.shape[1] // step, one_chunk, 0)
    mine = lax.axis_index("view")
    total = jnp.zeros((1, min(slot_cap, LANES)), F32)
    for peer in range(peers):
        same = ((peer // sub_count) % view_count == mine).astype(F32)
        total = total + same * back_ref[packet.extra(peer)]
    appear_ref[...] = (total * (1.0 / pixels))[:, :12]


def exchange_kernel(view_count, sub_count, in_ref, out_ref, send_sem, recv_sem, own_sem):
    peers = in_ref.shape[0]
    me = (lax.axis_index("tile") * view_count + lax.axis_index("view")) * sub_count
    me = me + lax.axis_index("sub")

    def device(number):
        return {
            "tile": number // (view_count * sub_count),
            "view": (number // sub_count) % view_count,
            "sub": number % sub_count,
        }

    barrier = pltpu.get_barrier_semaphore()
    for offset in range(1, peers):
        pl.semaphore_signal(
            barrier,
            inc=1,
            device_id=device((me + offset) % peers),
            device_id_type=pl.DeviceIdType.MESH,
        )
    own = pltpu.make_async_copy(in_ref.at[me], out_ref.at[me], own_sem)
    own.start()
    pl.semaphore_wait(barrier, peers - 1)
    copies = []
    for offset in sorted(range(1, peers), key=lambda n: abs(2 * n - peers)):
        dest = (me + offset) % peers
        copy = pltpu.make_async_remote_copy(
            src_ref=in_ref.at[dest],
            dst_ref=out_ref.at[me],
            send_sem=send_sem.at[offset],
            recv_sem=recv_sem.at[offset],
            device_id=device(dest),
            device_id_type=pl.DeviceIdType.MESH,
        )
        copy.start()
        copies.append(copy)
    own.wait()
    for copy in copies:
        copy.wait()


def exchange(packets, number, peers, slot_cap):
    view_count = lax.axis_size("view")
    sub_count = lax.axis_size("sub")
    if slot_cap % LANES:
        blocks = packets.shape[0]
        rows = packets[:, :10].transpose(1, 0, 2).reshape(10, blocks * LANES)
        rows = lax.all_to_all(rows, ROUTE_AXES, split_axis=1, concat_axis=1, tiled=True)
        rows = rows.reshape(10, blocks, LANES).transpose(1, 0, 2)
        return jnp.pad(rows, ((0, 0), (0, 6), (0, 0)))
    return pl.pallas_call(
        functools.partial(exchange_kernel, view_count, sub_count),
        out_shape=jax.ShapeDtypeStruct(packets.shape, F32),
        in_specs=[IN_VMEM],
        out_specs=IN_VMEM,
        scratch_shapes=[
            pltpu.SemaphoreType.DMA((peers,)),
            pltpu.SemaphoreType.DMA((peers,)),
            pltpu.SemaphoreType.DMA,
        ],
        compiler_params=pltpu.CompilerParams(collective_id=number, has_side_effects=True),
        name="exchange",
    )(packets)


def on_device(
    centers,
    scale_log,
    shear_terms,
    opacity_logit,
    sh_coeffs,
    cameras,
    appearance,
    target,
    send_index,
    send_count,
    tile_list,
    tile_count,
):
    peers, slot_cap = send_index.shape[1:]
    slots = peers * slot_cap
    blocks = slots // LANES
    gauss_count = centers.shape[1]
    tiles, list_len = tile_list.shape[1:]
    tile_pix = target.shape[-1]
    sub_count = lax.axis_size("sub")
    view_count = lax.axis_size("view")
    tile_devs = lax.axis_size("tile")
    harmonics = harmonic_table(cameras)
    opacity_row = opacity_logit[None, :]
    source = (centers, scale_log, shear_terms, opacity_row)
    deep = max(slot_cap // LANES, 1)
    packet_shape = jax.ShapeDtypeStruct((blocks // deep, 8 * deep + 8, LANES), F32)
    if slot_cap % LANES:
        slot_rows = send_index.reshape(blocks, LANES)
    else:
        slot_rows = send_index[0]
    outgoing, place, owner = pl.pallas_call(
        functools.partial(owner_kernel, sub_count, view_count, slot_cap),
        out_shape=(
            packet_shape,
            jax.ShapeDtypeStruct((2 * blocks, LANES), I32),
            jax.ShapeDtypeStruct((8, gauss_count), F32),
        ),
        in_specs=[IN_VMEM] * 5 + [IN_SMEM, IN_VMEM, IN_VMEM, IN_SMEM],
        out_specs=(IN_VMEM,) * 3,
        scratch_shapes=[
            pltpu.VMEM((blocks, LANES), I32),
            pltpu.VMEM((blocks, LANES), I32),
            pltpu.VMEM((16, gauss_count), F32),
        ],
        compiler_params=PARAMS,
        name="owner_rows",
    )(*source, sh_coeffs, cameras, harmonics, slot_rows, send_count)
    arrived = exchange(outgoing, 0, peers, slot_cap)
    returning, rendered = pl.pallas_call(
        functools.partial(tile_kernel, slot_cap, peers, sub_count),
        out_shape=(
            packet_shape,
            jax.ShapeDtypeStruct((3, tiles, tile_pix), F32),
        ),
        in_specs=[IN_VMEM, IN_VMEM, IN_SMEM, IN_SMEM, IN_VMEM],
        out_specs=(IN_VMEM,) * 2,
        scratch_shapes=[
            pltpu.VMEM((9 * list_len // LANES, tiles, LANES), F32),
            pltpu.VMEM((list_len, tiles, tile_pix), F32),
            pltpu.VMEM((list_len, tiles, tile_pix), F32),
            pltpu.VMEM((16, tiles * list_len), F32),
            pltpu.VMEM((blocks, LANES), I32),
            pltpu.VMEM((blocks, LANES), I32),
        ],
        compiler_params=PARAMS,
        name="tile_blend",
    )(arrived, tile_list[0], tile_count, appearance, target[:, 0, 0])
    returned = exchange(returning, 1, peers, slot_cap)
    param_grad, appearance_grad = pl.pallas_call(
        functools.partial(
            gradient_kernel,
            sub_count,
            view_count,
            slot_cap,
            peers,
            float(tile_devs * sub_count * tiles * tile_pix),
        ),
        out_shape=(
            jax.ShapeDtypeStruct((10 + sh_coeffs.shape[0], gauss_count), F32),
            jax.ShapeDtypeStruct((1, 12), F32),
        ),
        in_specs=[IN_VMEM] * 4 + [IN_SMEM] + [IN_VMEM] * 4,
        out_specs=(IN_VMEM,) * 2,
        scratch_shapes=[
            pltpu.VMEM((16, gauss_count), F32),
            pltpu.VMEM((blocks, LANES), I32),
            pltpu.VMEM((blocks, LANES), I32),
        ],
        compiler_params=PARAMS,
        name="owner_gradient",
    )(*source, cameras, harmonics, place, owner, returned)
    return (rendered[:, None, None], param_grad, appearance_grad)


def solution(mesh):
    return jax.shard_map(
        on_device,
        mesh=mesh,
        in_specs=(
            P(None, ("group", "tile", "view", "sub")),
            P(None, ("group", "tile", "view", "sub")),
            P(None, ("group", "tile", "view", "sub")),
            P(("group", "tile", "view", "sub")),
            P(None, ("group", "tile", "view", "sub")),
            P("group", None),
            P(("group", "view"), None),
            P(None, ("group", "view"), ("tile", "sub"), None, None),
            P(("group", "tile", "view", "sub"), None, None),
            P(("group", "tile", "view", "sub"), None),
            P(("group", "tile", "view", "sub"), None, None),
            P(("group", "tile", "view", "sub"), None),
        ),
        out_specs=(
            P(None, ("group", "view"), ("tile", "sub"), None, None),
            P(None, ("group", "tile", "view", "sub")),
            P(("group", "view"), None),
        ),
        check_vma=False,
    )
```

```python
import functools

import jax
import jax.numpy as jnp
from jax import lax
from jax.experimental import pallas as pl
from jax.experimental.pallas import tpu as pltpu
from jax.sharding import PartitionSpec as P

F32 = jnp.float32
BF16 = jnp.bfloat16
I32 = jnp.int32
LOG2E = 1.4426950408889634
LANES = 128
ROUTE_AXES = ("tile", "view", "sub")
NT = (((1,), (1,)), ((), ()))
PARAMS = pltpu.CompilerParams(vmem_limit_bytes=48 * 1024 * 1024)
IN_VMEM = pl.BlockSpec(memory_space=pltpu.VMEM)
IN_PLACE = pl.BlockSpec(memory_space=pl.ANY)
IN_SMEM = pl.BlockSpec(memory_space=pltpu.SMEM)


def harmonic_table(cameras):
    polar_angle = cameras[:, 6]
    azimuth = cameras[:, 7]
    unit_x = jnp.sin(polar_angle) * jnp.cos(azimuth)
    unit_y = jnp.sin(polar_angle) * jnp.sin(azimuth)
    unit_z = jnp.cos(polar_angle)
    square_x = unit_x * unit_x
    square_y = unit_y * unit_y
    square_z = unit_z * unit_z
    columns = [
        jnp.full_like(unit_x, 0.28209479177387814),
        -0.4886025119029199 * unit_y,
        0.4886025119029199 * unit_z,
        -0.4886025119029199 * unit_x,
        1.0925484305920792 * unit_x * unit_y,
        -1.0925484305920792 * unit_y * unit_z,
        0.31539156525252005 * (2.0 * square_z - square_x - square_y),
        -1.0925484305920792 * unit_x * unit_z,
        0.5462742152960396 * (square_x - square_y),
        -0.5900435899266435 * unit_y * (3.0 * square_x - square_y),
        2.890611442640554 * unit_x * unit_y * unit_z,
        -0.4570457994644658 * unit_y * (4.0 * square_z - square_x - square_y),
        0.3731763325901154 * unit_z * (2.0 * square_z - 3.0 * square_x - 3.0 * square_y),
        -0.4570457994644658 * unit_x * (4.0 * square_z - square_x - square_y),
        1.445305721320277 * unit_z * (square_x - square_y),
        -0.5900435899266435 * unit_x * (square_x - 3.0 * square_y),
    ]
    return jnp.stack(columns, axis=0)


def project_shape(p0, p1, p2, p3, p4, p5, p6, p7, p8, camera):
    focal_x, skew_x, center_x, focal_y, skew_y, center_y = camera
    mean_x = focal_x * p0 + skew_x * p2 + center_x
    mean_y = focal_y * p1 + skew_y * p2 + center_y
    factor_xx = jnp.exp(p3)
    factor_yy = jnp.exp(p4)
    factor_zz = jnp.exp(p5)
    factor_yx = p6 * factor_xx
    factor_zx = p7 * factor_xx
    factor_zy = p8 * factor_yy
    upper_x = focal_x * factor_xx + skew_x * factor_zx
    upper_y = skew_x * factor_zy
    upper_z = skew_x * factor_zz
    below_x = focal_y * factor_yx + skew_y * factor_zx
    below_y = focal_y * factor_yy + skew_y * factor_zy
    below_z = skew_y * factor_zz
    spread_xx = upper_x * upper_x + upper_y * upper_y + upper_z * upper_z + 0.3
    spread_xy = upper_x * below_x + upper_y * below_y + upper_z * below_z
    spread_yy = below_x * below_x + below_y * below_y + below_z * below_z + 0.3
    inverse = 1.0 / (spread_xx * spread_yy - spread_xy * spread_xy)
    return (mean_x, mean_y, spread_yy * inverse, -spread_xy * inverse, spread_xx * inverse)


def lane_gather(values, lanes):
    dims = lax.GatherDimensionNumbers(
        offset_dims=(),
        collapsed_slice_dims=(1,),
        start_index_map=(1,),
        operand_batching_dims=(0,),
        start_indices_batching_dims=(0,),
    )
    return lax.gather(
        values,
        lanes[:, :, None],
        dims,
        slice_sizes=(1, 1),
        mode=lax.GatherScatterMode.PROMISE_IN_BOUNDS,
    )


def spread(row, rows):
    return jnp.broadcast_to(row, (rows, row.shape[1]))


def iota(shape, dim):
    return lax.broadcasted_iota(I32, shape, dim)


def divide(values, number):
    if number & (number - 1) == 0:
        return values >> (number.bit_length() - 1)
    return lax.div(values, jnp.full_like(values, number))


def inverse_table(blocks, items):
    total = jnp.zeros((2 * blocks, LANES), F32)
    group = 8
    for start in range(0, len(items), group):
        lefts, rights = [], []
        for high, low, first, second, live in items[start : start + group]:
            hit = iota((blocks, LANES), 0) == high
            if live is not None:
                hit = jnp.logical_and(hit, live)
            lefts.append(
                jnp.concatenate([jnp.where(hit, first, 0.0), jnp.where(hit, second, 0.0)], axis=0)
            )
            rights.append((iota((LANES, LANES), 0) == low).astype(F32))
        left = jnp.concatenate(lefts, axis=1).astype(BF16)
        right = jnp.concatenate(rights, axis=1).astype(BF16)
        total = total + lax.dot_general(left, right, NT, preferred_element_type=F32)
    return total.astype(I32)


def gather_columns(high_ref, low_ref, blocks, tile_of, ninth_of, finish, finish_ninth):
    places = high_ref.shape[0]
    together = 4
    for group in range(places // 8):
        high = high_ref[group * 8 : group * 8 + 8, :]
        low = low_ref[group * 8 : group * 8 + 8, :]
        found = jnp.zeros((8, LANES), F32)
        for block in range(blocks):
            found = jnp.where(high == block, lane_gather(spread(ninth_of(block), 8), low), found)
        for inner in range(8):
            finish_ninth(group * 8 + inner, found[inner : inner + 1, :])

    def some_blocks(number, carry):
        first = number * together
        high = [spread(high_ref[pl.ds(first + n, 1), :], 8) for n in range(together)]
        low = [spread(low_ref[pl.ds(first + n, 1), :], 8) for n in range(together)]
        found = [jnp.zeros((8, LANES), F32) for _ in range(together)]
        for block in range(blocks):
            values = tile_of(block)
            for n in range(together):
                found[n] = jnp.where(high[n] == block, lane_gather(values, low[n]), found[n])
        for n in range(together):
            finish(first + n, found[n], low[n])
        return carry

    lax.fori_loop(0, places // together, some_blocks, 0)


class Packet:
    def __init__(self, ref, slot_cap):
        self.ref = ref
        self.cap = slot_cap
        self.deep = max(slot_cap // LANES, 1)

    def tile(self, block):
        start = (block % self.deep) * 8
        if not isinstance(block, int):
            start = pl.multiple_of(start, 8)
        return (block // self.deep, pl.ds(start, 8), slice(None))

    def row(self, block, number):
        start = (block % self.deep) * 8 + number if number < 8 else self.deep * 8 + block % self.deep
        return (block // self.deep, slice(start, start + 1), slice(None))

    def extra(self, peer):
        start = peer * self.cap
        lanes = slice(start % LANES, start % LANES + min(self.cap, LANES))
        return (start // LANES // self.deep, slice(9 * self.deep, 9 * self.deep + 1), lanes)


def select_camera(cameras_ref, view):
    chosen = []
    for column in range(6):
        value = jnp.full(view.shape, cameras_ref[0, column], F32)
        for other in range(1, cameras_ref.shape[0]):
            value = jnp.where(view == other, cameras_ref[other, column], value)
        chosen.append(value)
    return chosen


def select_harmonics(harmonics_ref, view):
    shape = (16, view.shape[1])
    value = jnp.broadcast_to(harmonics_ref[:, 0:1], shape)
    for other in range(1, harmonics_ref.shape[1]):
        value = jnp.where(
            view == other, jnp.broadcast_to(harmonics_ref[:, other : other + 1], shape), value
        )
    return value


def owner_kernel(
    sub_count,
    view_count,
    slot_cap,
    centers_in,
    scale_in,
    shear_in,
    opacity_in,
    coeff_in,
    cameras_ref,
    harmonics_ref,
    slots_ref,
    count_ref,
    out_ref,
    place_ref,
    owner_ref,
    high_ref,
    low_ref,
    projected_ref,
    centers_ref,
    scale_ref,
    shear_ref,
    opacity_ref,
    coeff_ref,
    load_sem,
):
    loads = [
        pltpu.make_async_copy(source, target, load_sem.at[number])
        for number, (source, target) in enumerate(
            (
                (coeff_in, coeff_ref),
                (centers_in, centers_ref),
                (scale_in, scale_ref),
                (shear_in, shear_ref),
                (opacity_in, opacity_ref),
            )
        )
    ]
    for load in loads:
        load.start()
    blocks = high_ref.shape[0]
    wide = slots_ref.shape[1] // LANES
    peers = count_ref.shape[1]
    packet = Packet(out_ref, slot_cap)
    lane = iota((1, LANES), 1).astype(F32)
    items = []
    for block in range(blocks):
        cut = slice((block % wide) * LANES, (block % wide + 1) * LANES)
        row = slots_ref[block // wide : block // wide + 1, cut]
        high = row >> 7
        low = row & 127
        high_ref[block : block + 1, :] = high
        low_ref[block : block + 1, :] = low
        items.append((high, low, float(block), lane, None))
    table = inverse_table(blocks, items)
    place_ref[...] = table
    position = table[0:blocks] * LANES + table[blocks:]
    dest = divide(position, slot_cap)
    view = lax.rem(divide(dest, sub_count), jnp.full_like(dest, view_count))
    within = position - dest * slot_cap
    limit = jnp.zeros_like(dest)
    for peer in range(peers):
        limit = jnp.where(dest == peer, count_ref[0, peer], limit)
    live = (within < limit).astype(F32)
    view = view.astype(F32)
    for block in range(blocks):
        cut = slice(block * LANES, (block + 1) * LANES)
        owner_ref[0:1, cut] = view[block : block + 1, :]
        owner_ref[1:2, cut] = live[block : block + 1, :]

    for load in loads:
        load.wait()
    step = 512

    def one_chunk(number, carry):
        cut = pl.ds(pl.multiple_of(number * step, step), step)
        view_row = owner_ref[0:1, cut]
        camera = select_camera(cameras_ref, view_row)
        params = [ref[r : r + 1, cut] for ref in (centers_ref, scale_ref, shear_ref) for r in range(3)]
        rows = list(project_shape(*params, camera))
        logit = opacity_ref[0:1, cut]
        rows.append(jnp.minimum(logit, 0.0) - jnp.log1p(jnp.exp(-jnp.abs(logit))))
        basis = select_harmonics(harmonics_ref, view_row)
        for color in range(3):
            terms = coeff_ref[color * 16 : color * 16 + 16, cut] * basis
            value = jnp.sum(terms, axis=0, keepdims=True) + 0.5
            slope = jnp.where(value > 0.0, 1.0, jnp.where(value == 0.0, 0.5, 0.0))
            owner_ref[2 + color : 3 + color, cut] = slope
            rows.append(jnp.maximum(value, 0.0))
        for row in range(9):
            projected_ref[row : row + 1, cut] = rows[row]
        return carry

    lax.fori_loop(0, coeff_ref.shape[1] // step, one_chunk, 0)

    def tile_of(block):
        return projected_ref[0:8, block * LANES : (block + 1) * LANES]

    def ninth_of(block):
        return projected_ref[8:9, block * LANES : (block + 1) * LANES]

    def finish(place, found, low):
        out_ref[packet.tile(place)] = found

    def finish_ninth(place, found):
        out_ref[packet.row(place, 8)] = found

    gather_columns(
        high_ref, low_ref, projected_ref.shape[1] // LANES, tile_of, ninth_of, finish, finish_ninth
    )
    for peer in range(peers):
        out_ref[packet.extra(peer)] = jnp.full(
            (1, min(slot_cap, LANES)), count_ref[0, peer].astype(F32)
        )


def tile_kernel(
    slot_cap,
    peers,
    sub_count,
    pool_ref,
    list_ref,
    count_ref,
    appear_ref,
    target_ref,
    out_ref,
    rendered_ref,
    entry_ref,
    alpha_ref,
    weight_ref,
    moment_ref,
    high_ref,
    low_ref,
):
    tiles, list_len = list_ref.shape
    tile_pix = target_ref.shape[2]
    blocks = high_ref.shape[0]
    pool = Packet(pool_ref, slot_cap)
    packet = Packet(out_ref, slot_cap)
    cols = list_len // LANES
    halves = tile_pix // LANES
    tile_row = lax.axis_index("tile") * sub_count + lax.axis_index("sub")
    center_y = 16.0 * tile_row.astype(F32) + 7.5

    entries = list_ref[...]
    column = entries
    inclusive = jnp.zeros((1, LANES), I32)
    for peer in range(peers):
        received = pool_ref[pool.extra(peer)]
        if slot_cap < LANES:
            received = jnp.broadcast_to(received[:, 0:1], (1, LANES))
        received = received.astype(I32)
        inclusive = inclusive + received
        bound = jnp.concatenate([spread(inclusive, tiles)] * cols, axis=1)
        gap = jnp.concatenate([spread(slot_cap - received, tiles)] * cols, axis=1)
        column = column + jnp.where(bound <= entries, gap, 0)
    column = jnp.clip(column, 0, blocks * LANES - 1)
    lane = iota((tiles, list_len), 1)
    tile = iota((tiles, list_len), 0)
    live_limit = jnp.zeros((tiles, list_len), I32)
    for number in range(tiles):
        live_limit = jnp.where(tile == number, count_ref[0, number], live_limit)
    live = lane < live_limit
    high_all = column >> 7
    low_all = column & 127

    tile_x = 16.0 * iota((tiles, LANES), 0).astype(F32) + 7.5
    for col in range(cols):
        cut = slice(col * LANES, (col + 1) * LANES)
        high = high_all[:, cut]
        low = low_all[:, cut]
        found = [jnp.zeros((tiles, LANES), F32) for _ in range(9)]
        for block in range(blocks):
            hit = high == block
            for row in range(9):
                source = spread(pool_ref[pool.row(block, row)], tiles)
                found[row] = jnp.where(hit, lane_gather(source, low), found[row])
        found[0] = found[0] - tile_x
        found[1] = found[1] - center_y
        found[2] = found[2] * (-0.5 * LOG2E)
        found[3] = found[3] * (-LOG2E)
        found[4] = found[4] * (-0.5 * LOG2E)
        found[5] = jnp.where(live[:, cut], found[5] * LOG2E, -1e30)
        for row in range(9):
            entry_ref[row * cols + col] = found[row]

    pixel = iota((tiles, LANES), 1)
    pixel_x = (pixel & 15).astype(F32) - 7.5
    pixel_y = [((pixel + half * LANES) >> 4).astype(F32) - 7.5 for half in range(halves)]

    state = (
        tuple(jnp.ones((tiles, LANES), F32) for _ in range(halves)),
        tuple(jnp.zeros((tiles, LANES), F32) for _ in range(3 * halves)),
    )
    for col in range(cols):

        def forward(k, state, col=col):
            transmit, colors = state
            at = jnp.full((tiles, LANES), k, I32)
            row = [lane_gather(entry_ref[r * cols + col], at) for r in range(9)]
            delta_x = row[0] - pixel_x
            part = row[2] * delta_x * delta_x + row[5]
            slope = row[3] * delta_x
            new_transmit = []
            new_colors = []
            for half in range(halves):
                delta_y = row[1] - pixel_y[half]
                alpha = jnp.exp2(part + delta_y * (slope + row[4] * delta_y))
                weight = alpha * transmit[half]
                cut = slice(half * LANES, (half + 1) * LANES)
                alpha_ref[col * LANES + k, :, cut] = alpha
                weight_ref[col * LANES + k, :, cut] = weight
                new_transmit.append(transmit[half] * (1.0 - alpha))
                for color in range(3):
                    new_colors.append(colors[half * 3 + color] + weight * row[6 + color])
            return (tuple(new_transmit), tuple(new_colors))

        state = lax.fori_loop(0, LANES, forward, state, unroll=32)
    blended = [
        jnp.concatenate([state[1][half * 3 + color] for half in range(halves)], axis=1)
        for color in range(3)
    ]

    mixing = [
        [appear_ref[0, 3 * c + d] + (1.0 if c == d else 0.0) for d in range(3)] for c in range(3)
    ]
    residue = []
    for c in range(3):
        value = appear_ref[0, 9 + c]
        value = (
            mixing[c][0] * blended[0] + mixing[c][1] * blended[1] + mixing[c][2] * blended[2] + value
        )
        rendered_ref[c] = value
        residue.append(value - target_ref[c])
    back = [
        mixing[0][d] * residue[0] + mixing[1][d] * residue[1] + mixing[2][d] * residue[2]
        for d in range(3)
    ]
    sums = [residue[c] * blended[d] for c in range(3) for d in range(3)] + residue
    term_lane = iota((1, min(slot_cap, LANES)), 1)
    term_row = jnp.zeros((1, min(slot_cap, LANES)), F32)
    for number, values in enumerate(sums):
        total = jnp.sum(jnp.sum(values, axis=0, keepdims=True), axis=1, keepdims=True)
        term_row = jnp.where(term_lane == number, total, term_row)

    back_half = [
        [back[c][:, half * LANES : (half + 1) * LANES] for c in range(3)] for half in range(halves)
    ]
    behind = tuple(jnp.zeros((tiles, LANES), F32) for _ in range(halves))
    for col in reversed(range(cols)):

        def backward(number, behind, col=col):
            k = LANES - 1 - number
            at = jnp.full((tiles, LANES), k, I32)
            row = [lane_gather(entry_ref[r * cols + col], at) for r in (6, 7, 8)]
            new_behind = []
            for half in range(halves):
                cut = slice(half * LANES, (half + 1) * LANES)
                seen = (
                    back_half[half][0] * row[0]
                    + back_half[half][1] * row[1]
                    + back_half[half][2] * row[2]
                )
                ahead = seen - behind[half]
                alpha = alpha_ref[col * LANES + k, :, cut]
                new_behind.append(behind[half] + alpha * ahead)
                alpha_ref[col * LANES + k, :, cut] = ahead * weight_ref[col * LANES + k, :, cut]
            return tuple(new_behind)

        behind = lax.fori_loop(0, LANES, backward, behind, unroll=32)

    pix = iota((16, tile_pix), 1)
    mono_x = (pix & 15).astype(F32) - 7.5
    mono_y = (pix >> 4).astype(F32) - 7.5
    kind = iota((16, tile_pix), 0)
    mono = jnp.where(kind == 0, 1.0, 0.0)
    for number, values in enumerate(
        (mono_x, mono_y, mono_x * mono_x, mono_x * mono_y, mono_y * mono_y)
    ):
        mono = jnp.where(kind == number + 1, values, mono)
    mono = mono.astype(BF16)
    back_all = jnp.concatenate(back, axis=0)
    back_high = back_all.astype(BF16)
    back_low = (back_all - back_high.astype(F32)).astype(BF16)
    back_both = jnp.concatenate([back_high, back_low], axis=0)
    steps = 32
    width = steps * tiles
    own_tile = iota((tiles, width), 0) == (iota((tiles, width), 1) & (tiles - 1))

    def reduce_pixels(number, carry):
        cut = pl.ds(pl.multiple_of(number * width, width), width)
        power = alpha_ref[pl.ds(number * steps, steps)].reshape(width, tile_pix)
        power_high = power.astype(BF16)
        power_low = (power - power_high.astype(F32)).astype(BF16)
        moments = lax.dot_general(mono, power_high, NT, preferred_element_type=F32)
        moments = moments + lax.dot_general(mono, power_low, NT, preferred_element_type=F32)
        moment_ref[0:8, cut] = moments[0:8]
        weight = weight_ref[pl.ds(number * steps, steps)].reshape(width, tile_pix)
        weight_high = weight.astype(BF16)
        weight_low = (weight - weight_high.astype(F32)).astype(BF16)
        colors = lax.dot_general(back_both, weight_high, NT, preferred_element_type=F32)
        colors = colors[: 3 * tiles] + colors[3 * tiles :]
        colors = colors + lax.dot_general(back_high, weight_low, NT, preferred_element_type=F32)
        for color in range(3):
            own = jnp.where(own_tile, colors[color * tiles : (color + 1) * tiles], 0.0)
            moment_ref[6 + color : 7 + color, cut] = jnp.sum(own, axis=0, keepdims=True)
        return carry

    lax.fori_loop(0, list_len // steps, reduce_pixels, 0)

    items = []
    place_lane = iota((1, LANES), 1)
    for number in range(tiles):
        for col in range(cols):
            cut = slice(col * LANES, (col + 1) * LANES)
            k = place_lane + col * LANES
            flat = k * tiles + number
            items.append(
                (
                    high_all[number : number + 1, cut],
                    low_all[number : number + 1, cut],
                    (flat >> 7).astype(F32),
                    (flat & 127).astype(F32),
                    k < count_ref[0, number],
                )
            )
    table = inverse_table(blocks, items)
    high_ref[...] = table[0:blocks]
    low_ref[...] = table[blocks:]

    def tile_of(block):
        return moment_ref[0:8, block * LANES : (block + 1) * LANES]

    def ninth_of(block):
        return moment_ref[8:9, block * LANES : (block + 1) * LANES]

    def finish(place, found, low):
        at = packet.tile(place)
        own = (low[0:1] & (tiles - 1)).astype(F32)
        shape = pool_ref[at]
        local_x = shape[0:1] - (16.0 * own + 7.5)
        local_y = shape[1:2] - center_y
        conic_a, conic_b, conic_c = shape[2:3], shape[3:4], shape[4:5]
        one, m_x, m_y, m_xx, m_xy, m_yy = [found[r : r + 1] for r in range(6)]
        d_x = local_x * one - m_x
        d_y = local_y * one - m_y
        d_xx = local_x * d_x - (local_x * m_x - m_xx)
        d_xy = local_y * d_x - (local_x * m_y - m_xy)
        d_yy = local_y * d_y - (local_y * m_y - m_yy)
        out_ref[at] = jnp.concatenate(
            [
                -(conic_a * d_x + conic_b * d_y),
                -(conic_c * d_y + conic_b * d_x),
                -0.5 * d_xx,
                -d_xy,
                -0.5 * d_yy,
                one,
                found[6:8],
            ],
            axis=0,
        )

    def finish_ninth(place, found):
        out_ref[packet.row(place, 8)] = found

    gather_columns(
        high_ref, low_ref, moment_ref.shape[1] // LANES, tile_of, ninth_of, finish, finish_ninth
    )
    for peer in range(peers):
        out_ref[packet.extra(peer)] = term_row


def gradient_kernel(
    sub_count,
    view_count,
    slot_cap,
    peers,
    pixels,
    centers_ref,
    scale_ref,
    shear_ref,
    opacity_ref,
    cameras_ref,
    harmonics_ref,
    place_ref,
    owner_ref,
    back_ref,
    out_ref,
    appear_ref,
    gathered_ref,
    high_ref,
    low_ref,
):
    blocks = high_ref.shape[0]
    packet = Packet(back_ref, slot_cap)
    high_ref[...] = place_ref[0:blocks, :]
    low_ref[...] = place_ref[blocks:, :]

    def tile_of(block):
        return back_ref[packet.tile(block)]

    def ninth_of(block):
        return back_ref[packet.row(block, 8)]

    def finish(place, found, low):
        gathered_ref[0:8, pl.ds(pl.multiple_of(place * LANES, LANES), LANES)] = found

    def finish_ninth(place, found):
        gathered_ref[8:9, place * LANES : (place + 1) * LANES] = found

    gather_columns(high_ref, low_ref, blocks, tile_of, ninth_of, finish, finish_ninth)
    step = 512

    def one_chunk(number, carry):
        cut = pl.ds(pl.multiple_of(number * step, step), step)
        view_row = owner_ref[0:1, cut]
        live = owner_ref[1:2, cut] > 0.0
        grads = [jnp.where(live, gathered_ref[r : r + 1, cut], 0.0) for r in range(9)]
        camera = select_camera(cameras_ref, view_row)
        params = [ref[r : r + 1, cut] for ref in (centers_ref, scale_ref, shear_ref) for r in range(3)]
        _, pullback = jax.vjp(lambda *rows: project_shape(*rows, camera), *params)
        for row, value in enumerate(pullback(tuple(grads[:5]))):
            out_ref[row : row + 1, cut] = value
        out_ref[9:10, cut] = grads[5] / (1.0 + jnp.exp(opacity_ref[0:1, cut]))
        basis = select_harmonics(harmonics_ref, view_row)
        for color in range(3):
            slope = owner_ref[2 + color : 3 + color, cut]
            out_ref[10 + 16 * color : 26 + 16 * color, cut] = basis * (slope * grads[6 + color])
        return carry

    lax.fori_loop(0, out_ref.shape[1] // step, one_chunk, 0)
    mine = lax.axis_index("view")
    total = jnp.zeros((1, min(slot_cap, LANES)), F32)
    for peer in range(peers):
        same = ((peer // sub_count) % view_count == mine).astype(F32)
        total = total + same * back_ref[packet.extra(peer)]
    appear_ref[...] = (total * (1.0 / pixels))[:, :12]


def exchange_kernel(view_count, sub_count, in_ref, out_ref, send_sem, recv_sem, own_sem):
    peers = in_ref.shape[0]
    me = (lax.axis_index("tile") * view_count + lax.axis_index("view")) * sub_count
    me = me + lax.axis_index("sub")

    def device(number):
        return {
            "tile": number // (view_count * sub_count),
            "view": (number // sub_count) % view_count,
            "sub": number % sub_count,
        }

    barrier = pltpu.get_barrier_semaphore()
    for offset in range(1, peers):
        pl.semaphore_signal(
            barrier,
            inc=1,
            device_id=device((me + offset) % peers),
            device_id_type=pl.DeviceIdType.MESH,
        )
    own = pltpu.make_async_copy(in_ref.at[me], out_ref.at[me], own_sem)
    own.start()
    pl.semaphore_wait(barrier, peers - 1)
    copies = []
    for offset in sorted(range(1, peers), key=lambda n: abs(2 * n - peers)):
        dest = (me + offset) % peers
        copy = pltpu.make_async_remote_copy(
            src_ref=in_ref.at[dest],
            dst_ref=out_ref.at[me],
            send_sem=send_sem.at[offset],
            recv_sem=recv_sem.at[offset],
            device_id=device(dest),
            device_id_type=pl.DeviceIdType.MESH,
        )
        copy.start()
        copies.append(copy)
    own.wait()
    for copy in copies:
        copy.wait()


def exchange(packets, number, peers, slot_cap):
    view_count = lax.axis_size("view")
    sub_count = lax.axis_size("sub")
    if slot_cap % LANES:
        blocks = packets.shape[0]
        rows = packets[:, :10].transpose(1, 0, 2).reshape(10, blocks * LANES)
        rows = lax.all_to_all(rows, ROUTE_AXES, split_axis=1, concat_axis=1, tiled=True)
        rows = rows.reshape(10, blocks, LANES).transpose(1, 0, 2)
        return jnp.pad(rows, ((0, 0), (0, 6), (0, 0)))
    return pl.pallas_call(
        functools.partial(exchange_kernel, view_count, sub_count),
        out_shape=jax.ShapeDtypeStruct(packets.shape, F32),
        in_specs=[IN_PLACE],
        out_specs=IN_PLACE,
        scratch_shapes=[
            pltpu.SemaphoreType.DMA((peers,)),
            pltpu.SemaphoreType.DMA((peers,)),
            pltpu.SemaphoreType.DMA,
        ],
        compiler_params=pltpu.CompilerParams(collective_id=number, has_side_effects=True),
        name="exchange",
    )(packets)


def on_device(
    centers,
    scale_log,
    shear_terms,
    opacity_logit,
    sh_coeffs,
    cameras,
    appearance,
    target,
    send_index,
    send_count,
    tile_list,
    tile_count,
):
    peers, slot_cap = send_index.shape[1:]
    slots = peers * slot_cap
    blocks = slots // LANES
    gauss_count = centers.shape[1]
    tiles, list_len = tile_list.shape[1:]
    tile_pix = target.shape[-1]
    sub_count = lax.axis_size("sub")
    view_count = lax.axis_size("view")
    tile_devs = lax.axis_size("tile")
    harmonics = harmonic_table(cameras)
    opacity_row = opacity_logit[None, :]
    source = (centers, scale_log, shear_terms, opacity_row)
    deep = max(slot_cap // LANES, 1)
    packet_shape = jax.ShapeDtypeStruct((blocks // deep, 8 * deep + 8, LANES), F32)
    if slot_cap % LANES:
        slot_rows = send_index.reshape(blocks, LANES)
    else:
        slot_rows = send_index[0]
    outgoing, place, owner = pl.pallas_call(
        functools.partial(owner_kernel, sub_count, view_count, slot_cap),
        out_shape=(
            packet_shape,
            jax.ShapeDtypeStruct((2 * blocks, LANES), I32),
            jax.ShapeDtypeStruct((8, gauss_count), F32),
        ),
        in_specs=[IN_PLACE] * 5 + [IN_SMEM, IN_VMEM, IN_VMEM, IN_SMEM],
        out_specs=(IN_VMEM,) * 3,
        scratch_shapes=[
            pltpu.VMEM((blocks, LANES), I32),
            pltpu.VMEM((blocks, LANES), I32),
            pltpu.VMEM((16, gauss_count), F32),
            pltpu.VMEM(centers.shape, F32),
            pltpu.VMEM(scale_log.shape, F32),
            pltpu.VMEM(shear_terms.shape, F32),
            pltpu.VMEM(opacity_row.shape, F32),
            pltpu.VMEM(sh_coeffs.shape, F32),
            pltpu.SemaphoreType.DMA((5,)),
        ],
        compiler_params=PARAMS,
        name="owner_rows",
    )(*source, sh_coeffs, cameras, harmonics, slot_rows, send_count)
    arrived = exchange(outgoing, 0, peers, slot_cap)
    returning, rendered = pl.pallas_call(
        functools.partial(tile_kernel, slot_cap, peers, sub_count),
        out_shape=(
            packet_shape,
            jax.ShapeDtypeStruct((3, tiles, tile_pix), F32),
        ),
        in_specs=[IN_VMEM, IN_VMEM, IN_SMEM, IN_SMEM, IN_VMEM],
        out_specs=(IN_VMEM,) * 2,
        scratch_shapes=[
            pltpu.VMEM((9 * list_len // LANES, tiles, LANES), F32),
            pltpu.VMEM((list_len, tiles, tile_pix), F32),
            pltpu.VMEM((list_len, tiles, tile_pix), F32),
            pltpu.VMEM((16, tiles * list_len), F32),
            pltpu.VMEM((blocks, LANES), I32),
            pltpu.VMEM((blocks, LANES), I32),
        ],
        compiler_params=PARAMS,
        name="tile_blend",
    )(arrived, tile_list[0], tile_count, appearance, target[:, 0, 0])
    returned = exchange(returning, 1, peers, slot_cap)
    param_grad, appearance_grad = pl.pallas_call(
        functools.partial(
            gradient_kernel,
            sub_count,
            view_count,
            slot_cap,
            peers,
            float(tile_devs * sub_count * tiles * tile_pix),
        ),
        out_shape=(
            jax.ShapeDtypeStruct((10 + sh_coeffs.shape[0], gauss_count), F32),
            jax.ShapeDtypeStruct((1, 12), F32),
        ),
        in_specs=[IN_VMEM] * 4 + [IN_SMEM] + [IN_VMEM] * 4,
        out_specs=(IN_VMEM,) * 2,
        scratch_shapes=[
            pltpu.VMEM((16, gauss_count), F32),
            pltpu.VMEM((blocks, LANES), I32),
            pltpu.VMEM((blocks, LANES), I32),
        ],
        compiler_params=PARAMS,
        name="owner_gradient",
    )(*source, cameras, harmonics, place, owner, returned)
    return (rendered[:, None, None], param_grad, appearance_grad)


def solution(mesh):
    return jax.shard_map(
        on_device,
        mesh=mesh,
        in_specs=(
            P(None, ("group", "tile", "view", "sub")),
            P(None, ("group", "tile", "view", "sub")),
            P(None, ("group", "tile", "view", "sub")),
            P(("group", "tile", "view", "sub")),
            P(None, ("group", "tile", "view", "sub")),
            P("group", None),
            P(("group", "view"), None),
            P(None, ("group", "view"), ("tile", "sub"), None, None),
            P(("group", "tile", "view", "sub"), None, None),
            P(("group", "tile", "view", "sub"), None),
            P(("group", "tile", "view", "sub"), None, None),
            P(("group", "tile", "view", "sub"), None),
        ),
        out_specs=(
            P(None, ("group", "view"), ("tile", "sub"), None, None),
            P(None, ("group", "tile", "view", "sub")),
            P(("group", "view"), None),
        ),
        check_vma=False,
    )
```

```python
import functools

import jax
import jax.numpy as jnp
from jax import lax
from jax.experimental import pallas as pl
from jax.experimental.pallas import tpu as pltpu
from jax.sharding import PartitionSpec as P

F32 = jnp.float32
BF16 = jnp.bfloat16
I32 = jnp.int32
LOG2E = 1.4426950408889634
LANES = 128
ROUTE_AXES = ("tile", "view", "sub")
NT = (((1,), (1,)), ((), ()))
PARAMS = pltpu.CompilerParams(vmem_limit_bytes=48 * 1024 * 1024)
IN_VMEM = pl.BlockSpec(memory_space=pltpu.VMEM)
IN_PLACE = pl.BlockSpec(memory_space=pltpu.HBM)
IN_SMEM = pl.BlockSpec(memory_space=pltpu.SMEM)


def harmonic_table(cameras):
    polar_angle = cameras[:, 6]
    azimuth = cameras[:, 7]
    unit_x = jnp.sin(polar_angle) * jnp.cos(azimuth)
    unit_y = jnp.sin(polar_angle) * jnp.sin(azimuth)
    unit_z = jnp.cos(polar_angle)
    square_x = unit_x * unit_x
    square_y = unit_y * unit_y
    square_z = unit_z * unit_z
    columns = [
        jnp.full_like(unit_x, 0.28209479177387814),
        -0.4886025119029199 * unit_y,
        0.4886025119029199 * unit_z,
        -0.4886025119029199 * unit_x,
        1.0925484305920792 * unit_x * unit_y,
        -1.0925484305920792 * unit_y * unit_z,
        0.31539156525252005 * (2.0 * square_z - square_x - square_y),
        -1.0925484305920792 * unit_x * unit_z,
        0.5462742152960396 * (square_x - square_y),
        -0.5900435899266435 * unit_y * (3.0 * square_x - square_y),
        2.890611442640554 * unit_x * unit_y * unit_z,
        -0.4570457994644658 * unit_y * (4.0 * square_z - square_x - square_y),
        0.3731763325901154 * unit_z * (2.0 * square_z - 3.0 * square_x - 3.0 * square_y),
        -0.4570457994644658 * unit_x * (4.0 * square_z - square_x - square_y),
        1.445305721320277 * unit_z * (square_x - square_y),
        -0.5900435899266435 * unit_x * (square_x - 3.0 * square_y),
    ]
    return jnp.stack(columns, axis=0)


def project_shape(p0, p1, p2, p3, p4, p5, p6, p7, p8, camera):
    focal_x, skew_x, center_x, focal_y, skew_y, center_y = camera
    mean_x = focal_x * p0 + skew_x * p2 + center_x
    mean_y = focal_y * p1 + skew_y * p2 + center_y
    factor_xx = jnp.exp(p3)
    factor_yy = jnp.exp(p4)
    factor_zz = jnp.exp(p5)
    factor_yx = p6 * factor_xx
    factor_zx = p7 * factor_xx
    factor_zy = p8 * factor_yy
    upper_x = focal_x * factor_xx + skew_x * factor_zx
    upper_y = skew_x * factor_zy
    upper_z = skew_x * factor_zz
    below_x = focal_y * factor_yx + skew_y * factor_zx
    below_y = focal_y * factor_yy + skew_y * factor_zy
    below_z = skew_y * factor_zz
    spread_xx = upper_x * upper_x + upper_y * upper_y + upper_z * upper_z + 0.3
    spread_xy = upper_x * below_x + upper_y * below_y + upper_z * below_z
    spread_yy = below_x * below_x + below_y * below_y + below_z * below_z + 0.3
    inverse = 1.0 / (spread_xx * spread_yy - spread_xy * spread_xy)
    return (mean_x, mean_y, spread_yy * inverse, -spread_xy * inverse, spread_xx * inverse)


def lane_gather(values, lanes):
    dims = lax.GatherDimensionNumbers(
        offset_dims=(),
        collapsed_slice_dims=(1,),
        start_index_map=(1,),
        operand_batching_dims=(0,),
        start_indices_batching_dims=(0,),
    )
    return lax.gather(
        values,
        lanes[:, :, None],
        dims,
        slice_sizes=(1, 1),
        mode=lax.GatherScatterMode.PROMISE_IN_BOUNDS,
    )


def spread(row, rows):
    return jnp.broadcast_to(row, (rows, row.shape[1]))


def iota(shape, dim):
    return lax.broadcasted_iota(I32, shape, dim)


def divide(values, number):
    if number & (number - 1) == 0:
        return values >> (number.bit_length() - 1)
    return lax.div(values, jnp.full_like(values, number))


def inverse_table(blocks, items):
    total = jnp.zeros((2 * blocks, LANES), F32)
    group = 8
    for start in range(0, len(items), group):
        lefts, rights = [], []
        for high, low, first, second, live in items[start : start + group]:
            hit = iota((blocks, LANES), 0) == high
            if live is not None:
                hit = jnp.logical_and(hit, live)
            lefts.append(
                jnp.concatenate([jnp.where(hit, first, 0.0), jnp.where(hit, second, 0.0)], axis=0)
            )
            rights.append((iota((LANES, LANES), 0) == low).astype(F32))
        left = jnp.concatenate(lefts, axis=1).astype(BF16)
        right = jnp.concatenate(rights, axis=1).astype(BF16)
        total = total + lax.dot_general(left, right, NT, preferred_element_type=F32)
    return total.astype(I32)


def gather_columns(high_ref, low_ref, blocks, tile_of, ninth_of, finish, finish_ninth):
    places = high_ref.shape[0]
    together = 4
    for group in range(places // 8):
        high = high_ref[group * 8 : group * 8 + 8, :]
        low = low_ref[group * 8 : group * 8 + 8, :]
        found = jnp.zeros((8, LANES), F32)
        for block in range(blocks):
            found = jnp.where(high == block, lane_gather(spread(ninth_of(block), 8), low), found)
        for inner in range(8):
            finish_ninth(group * 8 + inner, found[inner : inner + 1, :])

    def some_blocks(number, carry):
        first = number * together
        high = [spread(high_ref[pl.ds(first + n, 1), :], 8) for n in range(together)]
        low = [spread(low_ref[pl.ds(first + n, 1), :], 8) for n in range(together)]
        found = [jnp.zeros((8, LANES), F32) for _ in range(together)]
        for block in range(blocks):
            values = tile_of(block)
            for n in range(together):
                found[n] = jnp.where(high[n] == block, lane_gather(values, low[n]), found[n])
        for n in range(together):
            finish(first + n, found[n], low[n])
        return carry

    lax.fori_loop(0, places // together, some_blocks, 0)


class Packet:
    def __init__(self, ref, slot_cap):
        self.ref = ref
        self.cap = slot_cap
        self.deep = max(slot_cap // LANES, 1)

    def tile(self, block):
        start = (block % self.deep) * 8
        if not isinstance(block, int):
            start = pl.multiple_of(start, 8)
        return (block // self.deep, pl.ds(start, 8), slice(None))

    def row(self, block, number):
        start = (block % self.deep) * 8 + number if number < 8 else self.deep * 8 + block % self.deep
        return (block // self.deep, slice(start, start + 1), slice(None))

    def extra(self, peer):
        start = peer * self.cap
        lanes = slice(start % LANES, start % LANES + min(self.cap, LANES))
        return (start // LANES // self.deep, slice(9 * self.deep, 9 * self.deep + 1), lanes)


def select_camera(cameras_ref, view):
    chosen = []
    for column in range(6):
        value = jnp.full(view.shape, cameras_ref[0, column], F32)
        for other in range(1, cameras_ref.shape[0]):
            value = jnp.where(view == other, cameras_ref[other, column], value)
        chosen.append(value)
    return chosen


def select_harmonics(harmonics_ref, view):
    shape = (16, view.shape[1])
    value = jnp.broadcast_to(harmonics_ref[:, 0:1], shape)
    for other in range(1, harmonics_ref.shape[1]):
        value = jnp.where(
            view == other, jnp.broadcast_to(harmonics_ref[:, other : other + 1], shape), value
        )
    return value


def owner_kernel(
    sub_count,
    view_count,
    slot_cap,
    centers_in,
    scale_in,
    shear_in,
    opacity_in,
    coeff_in,
    cameras_ref,
    harmonics_ref,
    slots_ref,
    count_ref,
    out_ref,
    place_ref,
    owner_ref,
    high_ref,
    low_ref,
    projected_ref,
    centers_ref,
    scale_ref,
    shear_ref,
    opacity_ref,
    coeff_ref,
    load_sem,
):
    loads = [
        pltpu.make_async_copy(source, target, load_sem.at[number])
        for number, (source, target) in enumerate(
            (
                (coeff_in, coeff_ref),
                (centers_in, centers_ref),
                (scale_in, scale_ref),
                (shear_in, shear_ref),
                (opacity_in, opacity_ref),
            )
        )
    ]
    for load in loads:
        load.start()
    blocks = high_ref.shape[0]
    wide = slots_ref.shape[1] // LANES
    peers = count_ref.shape[1]
    packet = Packet(out_ref, slot_cap)
    lane = iota((1, LANES), 1).astype(F32)
    items = []
    for block in range(blocks):
        cut = slice((block % wide) * LANES, (block % wide + 1) * LANES)
        row = slots_ref[block // wide : block // wide + 1, cut]
        high = row >> 7
        low = row & 127
        high_ref[block : block + 1, :] = high
        low_ref[block : block + 1, :] = low
        items.append((high, low, float(block), lane, None))
    table = inverse_table(blocks, items)
    place_ref[...] = table
    position = table[0:blocks] * LANES + table[blocks:]
    dest = divide(position, slot_cap)
    view = lax.rem(divide(dest, sub_count), jnp.full_like(dest, view_count))
    within = position - dest * slot_cap
    limit = jnp.zeros_like(dest)
    for peer in range(peers):
        limit = jnp.where(dest == peer, count_ref[0, peer], limit)
    live = (within < limit).astype(F32)
    view = view.astype(F32)
    for block in range(blocks):
        cut = slice(block * LANES, (block + 1) * LANES)
        owner_ref[0:1, cut] = view[block : block + 1, :]
        owner_ref[1:2, cut] = live[block : block + 1, :]

    for load in loads:
        load.wait()
    step = 512

    def one_chunk(number, carry):
        cut = pl.ds(pl.multiple_of(number * step, step), step)
        view_row = owner_ref[0:1, cut]
        camera = select_camera(cameras_ref, view_row)
        params = [ref[r : r + 1, cut] for ref in (centers_ref, scale_ref, shear_ref) for r in range(3)]
        rows = list(project_shape(*params, camera))
        logit = opacity_ref[0:1, cut]
        rows.append(jnp.minimum(logit, 0.0) - jnp.log1p(jnp.exp(-jnp.abs(logit))))
        basis = select_harmonics(harmonics_ref, view_row)
        for color in range(3):
            terms = coeff_ref[color * 16 : color * 16 + 16, cut] * basis
            value = jnp.sum(terms, axis=0, keepdims=True) + 0.5
            slope = jnp.where(value > 0.0, 1.0, jnp.where(value == 0.0, 0.5, 0.0))
            owner_ref[2 + color : 3 + color, cut] = slope
            rows.append(jnp.maximum(value, 0.0))
        for row in range(9):
            projected_ref[row : row + 1, cut] = rows[row]
        return carry

    lax.fori_loop(0, coeff_ref.shape[1] // step, one_chunk, 0)

    def tile_of(block):
        return projected_ref[0:8, block * LANES : (block + 1) * LANES]

    def ninth_of(block):
        return projected_ref[8:9, block * LANES : (block + 1) * LANES]

    def finish(place, found, low):
        out_ref[packet.tile(place)] = found

    def finish_ninth(place, found):
        out_ref[packet.row(place, 8)] = found

    gather_columns(
        high_ref, low_ref, projected_ref.shape[1] // LANES, tile_of, ninth_of, finish, finish_ninth
    )
    for peer in range(peers):
        out_ref[packet.extra(peer)] = jnp.full(
            (1, min(slot_cap, LANES)), count_ref[0, peer].astype(F32)
        )


def tile_kernel(
    slot_cap,
    peers,
    sub_count,
    pool_ref,
    list_ref,
    count_ref,
    appear_ref,
    target_ref,
    out_ref,
    rendered_ref,
    entry_ref,
    alpha_ref,
    weight_ref,
    moment_ref,
    high_ref,
    low_ref,
):
    tiles, list_len = list_ref.shape
    tile_pix = target_ref.shape[2]
    blocks = high_ref.shape[0]
    pool = Packet(pool_ref, slot_cap)
    packet = Packet(out_ref, slot_cap)
    cols = list_len // LANES
    halves = tile_pix // LANES
    tile_row = lax.axis_index("tile") * sub_count + lax.axis_index("sub")
    center_y = 16.0 * tile_row.astype(F32) + 7.5

    entries = list_ref[...]
    column = entries
    inclusive = jnp.zeros((1, LANES), I32)
    for peer in range(peers):
        received = pool_ref[pool.extra(peer)]
        if slot_cap < LANES:
            received = jnp.broadcast_to(received[:, 0:1], (1, LANES))
        received = received.astype(I32)
        inclusive = inclusive + received
        bound = jnp.concatenate([spread(inclusive, tiles)] * cols, axis=1)
        gap = jnp.concatenate([spread(slot_cap - received, tiles)] * cols, axis=1)
        column = column + jnp.where(bound <= entries, gap, 0)
    column = jnp.clip(column, 0, blocks * LANES - 1)
    lane = iota((tiles, list_len), 1)
    tile = iota((tiles, list_len), 0)
    live_limit = jnp.zeros((tiles, list_len), I32)
    for number in range(tiles):
        live_limit = jnp.where(tile == number, count_ref[0, number], live_limit)
    live = lane < live_limit
    high_all = column >> 7
    low_all = column & 127

    tile_x = 16.0 * iota((tiles, LANES), 0).astype(F32) + 7.5
    for col in range(cols):
        cut = slice(col * LANES, (col + 1) * LANES)
        high = high_all[:, cut]
        low = low_all[:, cut]
        found = [jnp.zeros((tiles, LANES), F32) for _ in range(9)]
        for block in range(blocks):
            hit = high == block
            for row in range(9):
                source = spread(pool_ref[pool.row(block, row)], tiles)
                found[row] = jnp.where(hit, lane_gather(source, low), found[row])
        found[0] = found[0] - tile_x
        found[1] = found[1] - center_y
        found[2] = found[2] * (-0.5 * LOG2E)
        found[3] = found[3] * (-LOG2E)
        found[4] = found[4] * (-0.5 * LOG2E)
        found[5] = jnp.where(live[:, cut], found[5] * LOG2E, -1e30)
        for row in range(9):
            entry_ref[row * cols + col] = found[row]

    pixel = iota((tiles, LANES), 1)
    pixel_x = (pixel & 15).astype(F32) - 7.5
    pixel_y = [((pixel + half * LANES) >> 4).astype(F32) - 7.5 for half in range(halves)]

    state = (
        tuple(jnp.ones((tiles, LANES), F32) for _ in range(halves)),
        tuple(jnp.zeros((tiles, LANES), F32) for _ in range(3 * halves)),
    )
    for col in range(cols):

        def forward(k, state, col=col):
            transmit, colors = state
            at = jnp.full((tiles, LANES), k, I32)
            row = [lane_gather(entry_ref[r * cols + col], at) for r in range(9)]
            delta_x = row[0] - pixel_x
            part = row[2] * delta_x * delta_x + row[5]
            slope = row[3] * delta_x
            new_transmit = []
            new_colors = []
            for half in range(halves):
                delta_y = row[1] - pixel_y[half]
                alpha = jnp.exp2(part + delta_y * (slope + row[4] * delta_y))
                weight = alpha * transmit[half]
                cut = slice(half * LANES, (half + 1) * LANES)
                alpha_ref[col * LANES + k, :, cut] = alpha
                weight_ref[col * LANES + k, :, cut] = weight
                new_transmit.append(transmit[half] * (1.0 - alpha))
                for color in range(3):
                    new_colors.append(colors[half * 3 + color] + weight * row[6 + color])
            return (tuple(new_transmit), tuple(new_colors))

        state = lax.fori_loop(0, LANES, forward, state, unroll=64)
    blended = [
        jnp.concatenate([state[1][half * 3 + color] for half in range(halves)], axis=1)
        for color in range(3)
    ]

    mixing = [
        [appear_ref[0, 3 * c + d] + (1.0 if c == d else 0.0) for d in range(3)] for c in range(3)
    ]
    residue = []
    for c in range(3):
        value = appear_ref[0, 9 + c]
        value = (
            mixing[c][0] * blended[0] + mixing[c][1] * blended[1] + mixing[c][2] * blended[2] + value
        )
        rendered_ref[c] = value
        residue.append(value - target_ref[c])
    back = [
        mixing[0][d] * residue[0] + mixing[1][d] * residue[1] + mixing[2][d] * residue[2]
        for d in range(3)
    ]
    sums = [residue[c] * blended[d] for c in range(3) for d in range(3)] + residue
    term_lane = iota((1, min(slot_cap, LANES)), 1)
    term_row = jnp.zeros((1, min(slot_cap, LANES)), F32)
    for number, values in enumerate(sums):
        total = jnp.sum(jnp.sum(values, axis=0, keepdims=True), axis=1, keepdims=True)
        term_row = jnp.where(term_lane == number, total, term_row)

    back_half = [
        [back[c][:, half * LANES : (half + 1) * LANES] for c in range(3)] for half in range(halves)
    ]
    behind = tuple(jnp.zeros((tiles, LANES), F32) for _ in range(halves))
    for col in reversed(range(cols)):

        def backward(number, behind, col=col):
            k = LANES - 1 - number
            at = jnp.full((tiles, LANES), k, I32)
            row = [lane_gather(entry_ref[r * cols + col], at) for r in (6, 7, 8)]
            new_behind = []
            for half in range(halves):
                cut = slice(half * LANES, (half + 1) * LANES)
                seen = (
                    back_half[half][0] * row[0]
                    + back_half[half][1] * row[1]
                    + back_half[half][2] * row[2]
                )
                ahead = seen - behind[half]
                alpha = alpha_ref[col * LANES + k, :, cut]
                new_behind.append(behind[half] + alpha * ahead)
                alpha_ref[col * LANES + k, :, cut] = ahead * weight_ref[col * LANES + k, :, cut]
            return tuple(new_behind)

        behind = lax.fori_loop(0, LANES, backward, behind, unroll=64)

    pix = iota((16, tile_pix), 1)
    mono_x = (pix & 15).astype(F32) - 7.5
    mono_y = (pix >> 4).astype(F32) - 7.5
    kind = iota((16, tile_pix), 0)
    mono = jnp.where(kind == 0, 1.0, 0.0)
    for number, values in enumerate(
        (mono_x, mono_y, mono_x * mono_x, mono_x * mono_y, mono_y * mono_y)
    ):
        mono = jnp.where(kind == number + 1, values, mono)
    mono = mono.astype(BF16)
    back_all = jnp.concatenate(back, axis=0)
    back_high = back_all.astype(BF16)
    back_low = (back_all - back_high.astype(F32)).astype(BF16)
    back_both = jnp.concatenate([back_high, back_low], axis=0)
    steps = 32
    width = steps * tiles
    own_tile = iota((tiles, width), 0) == (iota((tiles, width), 1) & (tiles - 1))

    def reduce_pixels(number, carry):
        cut = pl.ds(pl.multiple_of(number * width, width), width)
        power = alpha_ref[pl.ds(number * steps, steps)].reshape(width, tile_pix)
        power_high = power.astype(BF16)
        power_low = (power - power_high.astype(F32)).astype(BF16)
        moments = lax.dot_general(mono, power_high, NT, preferred_element_type=F32)
        moments = moments + lax.dot_general(mono, power_low, NT, preferred_element_type=F32)
        moment_ref[0:8, cut] = moments[0:8]
        weight = weight_ref[pl.ds(number * steps, steps)].reshape(width, tile_pix)
        weight_high = weight.astype(BF16)
        weight_low = (weight - weight_high.astype(F32)).astype(BF16)
        colors = lax.dot_general(back_both, weight_high, NT, preferred_element_type=F32)
        colors = colors[: 3 * tiles] + colors[3 * tiles :]
        colors = colors + lax.dot_general(back_high, weight_low, NT, preferred_element_type=F32)
        for color in range(3):
            own = jnp.where(own_tile, colors[color * tiles : (color + 1) * tiles], 0.0)
            moment_ref[6 + color : 7 + color, cut] = jnp.sum(own, axis=0, keepdims=True)
        return carry

    lax.fori_loop(0, list_len // steps, reduce_pixels, 0)

    items = []
    place_lane = iota((1, LANES), 1)
    for number in range(tiles):
        for col in range(cols):
            cut = slice(col * LANES, (col + 1) * LANES)
            k = place_lane + col * LANES
            flat = k * tiles + number
            items.append(
                (
                    high_all[number : number + 1, cut],
                    low_all[number : number + 1, cut],
                    (flat >> 7).astype(F32),
                    (flat & 127).astype(F32),
                    k < count_ref[0, number],
                )
            )
    table = inverse_table(blocks, items)
    high_ref[...] = table[0:blocks]
    low_ref[...] = table[blocks:]

    def tile_of(block):
        return moment_ref[0:8, block * LANES : (block + 1) * LANES]

    def ninth_of(block):
        return moment_ref[8:9, block * LANES : (block + 1) * LANES]

    def finish(place, found, low):
        at = packet.tile(place)
        own = (low[0:1] & (tiles - 1)).astype(F32)
        shape = pool_ref[at]
        local_x = shape[0:1] - (16.0 * own + 7.5)
        local_y = shape[1:2] - center_y
        conic_a, conic_b, conic_c = shape[2:3], shape[3:4], shape[4:5]
        one, m_x, m_y, m_xx, m_xy, m_yy = [found[r : r + 1] for r in range(6)]
        d_x = local_x * one - m_x
        d_y = local_y * one - m_y
        d_xx = local_x * d_x - (local_x * m_x - m_xx)
        d_xy = local_y * d_x - (local_x * m_y - m_xy)
        d_yy = local_y * d_y - (local_y * m_y - m_yy)
        out_ref[at] = jnp.concatenate(
            [
                -(conic_a * d_x + conic_b * d_y),
                -(conic_c * d_y + conic_b * d_x),
                -0.5 * d_xx,
                -d_xy,
                -0.5 * d_yy,
                one,
                found[6:8],
            ],
            axis=0,
        )

    def finish_ninth(place, found):
        out_ref[packet.row(place, 8)] = found

    gather_columns(
        high_ref, low_ref, moment_ref.shape[1] // LANES, tile_of, ninth_of, finish, finish_ninth
    )
    for peer in range(peers):
        out_ref[packet.extra(peer)] = term_row


def gradient_kernel(
    sub_count,
    view_count,
    slot_cap,
    peers,
    pixels,
    centers_ref,
    scale_ref,
    shear_ref,
    opacity_ref,
    cameras_ref,
    harmonics_ref,
    place_ref,
    owner_ref,
    back_ref,
    out_ref,
    appear_ref,
    gathered_ref,
    high_ref,
    low_ref,
):
    blocks = high_ref.shape[0]
    packet = Packet(back_ref, slot_cap)
    high_ref[...] = place_ref[0:blocks, :]
    low_ref[...] = place_ref[blocks:, :]

    def tile_of(block):
        return back_ref[packet.tile(block)]

    def ninth_of(block):
        return back_ref[packet.row(block, 8)]

    def finish(place, found, low):
        gathered_ref[0:8, pl.ds(pl.multiple_of(place * LANES, LANES), LANES)] = found

    def finish_ninth(place, found):
        gathered_ref[8:9, place * LANES : (place + 1) * LANES] = found

    gather_columns(high_ref, low_ref, blocks, tile_of, ninth_of, finish, finish_ninth)
    step = 512

    def one_chunk(number, carry):
        cut = pl.ds(pl.multiple_of(number * step, step), step)
        view_row = owner_ref[0:1, cut]
        live = owner_ref[1:2, cut] > 0.0
        grads = [jnp.where(live, gathered_ref[r : r + 1, cut], 0.0) for r in range(9)]
        camera = select_camera(cameras_ref, view_row)
        params = [ref[r : r + 1, cut] for ref in (centers_ref, scale_ref, shear_ref) for r in range(3)]
        _, pullback = jax.vjp(lambda *rows: project_shape(*rows, camera), *params)
        for row, value in enumerate(pullback(tuple(grads[:5]))):
            out_ref[row : row + 1, cut] = value
        out_ref[9:10, cut] = grads[5] / (1.0 + jnp.exp(opacity_ref[0:1, cut]))
        basis = select_harmonics(harmonics_ref, view_row)
        for color in range(3):
            slope = owner_ref[2 + color : 3 + color, cut]
            out_ref[10 + 16 * color : 26 + 16 * color, cut] = basis * (slope * grads[6 + color])
        return carry

    lax.fori_loop(0, out_ref.shape[1] // step, one_chunk, 0)
    mine = lax.axis_index("view")
    total = jnp.zeros((1, min(slot_cap, LANES)), F32)
    for peer in range(peers):
        same = ((peer // sub_count) % view_count == mine).astype(F32)
        total = total + same * back_ref[packet.extra(peer)]
    appear_ref[...] = (total * (1.0 / pixels))[:, :12]


def exchange_kernel(view_count, sub_count, in_ref, out_ref, send_sem, recv_sem, own_sem):
    peers = in_ref.shape[0]
    me = (lax.axis_index("tile") * view_count + lax.axis_index("view")) * sub_count
    me = me + lax.axis_index("sub")

    def device(number):
        return {
            "tile": number // (view_count * sub_count),
            "view": (number // sub_count) % view_count,
            "sub": number % sub_count,
        }

    barrier = pltpu.get_barrier_semaphore()
    for offset in range(1, peers):
        pl.semaphore_signal(
            barrier,
            inc=1,
            device_id=device((me + offset) % peers),
            device_id_type=pl.DeviceIdType.MESH,
        )
    own = pltpu.make_async_copy(in_ref.at[me], out_ref.at[me], own_sem)
    own.start()
    pl.semaphore_wait(barrier, peers - 1)
    copies = []
    for offset in sorted(range(1, peers), key=lambda n: abs(2 * n - peers)):
        dest = (me + offset) % peers
        copy = pltpu.make_async_remote_copy(
            src_ref=in_ref.at[dest],
            dst_ref=out_ref.at[me],
            send_sem=send_sem.at[offset],
            recv_sem=recv_sem.at[offset],
            device_id=device(dest),
            device_id_type=pl.DeviceIdType.MESH,
        )
        copy.start()
        copies.append(copy)
    own.wait()
    for copy in copies:
        copy.wait()


def exchange(packets, number, peers, slot_cap):
    view_count = lax.axis_size("view")
    sub_count = lax.axis_size("sub")
    if slot_cap % LANES:
        blocks = packets.shape[0]
        rows = packets[:, :10].transpose(1, 0, 2).reshape(10, blocks * LANES)
        rows = lax.all_to_all(rows, ROUTE_AXES, split_axis=1, concat_axis=1, tiled=True)
        rows = rows.reshape(10, blocks, LANES).transpose(1, 0, 2)
        return jnp.pad(rows, ((0, 0), (0, 6), (0, 0)))
    return pl.pallas_call(
        functools.partial(exchange_kernel, view_count, sub_count),
        out_shape=jax.ShapeDtypeStruct(packets.shape, F32),
        in_specs=[IN_PLACE],
        out_specs=IN_PLACE,
        scratch_shapes=[
            pltpu.SemaphoreType.DMA((peers,)),
            pltpu.SemaphoreType.DMA((peers,)),
            pltpu.SemaphoreType.DMA,
        ],
        compiler_params=pltpu.CompilerParams(collective_id=number, has_side_effects=True),
        name="exchange",
    )(packets)


def on_device(
    centers,
    scale_log,
    shear_terms,
    opacity_logit,
    sh_coeffs,
    cameras,
    appearance,
    target,
    send_index,
    send_count,
    tile_list,
    tile_count,
):
    peers, slot_cap = send_index.shape[1:]
    slots = peers * slot_cap
    blocks = slots // LANES
    gauss_count = centers.shape[1]
    tiles, list_len = tile_list.shape[1:]
    tile_pix = target.shape[-1]
    sub_count = lax.axis_size("sub")
    view_count = lax.axis_size("view")
    tile_devs = lax.axis_size("tile")
    harmonics = harmonic_table(cameras)
    opacity_row = opacity_logit[None, :]
    source = (centers, scale_log, shear_terms, opacity_row)
    deep = max(slot_cap // LANES, 1)
    packet_shape = jax.ShapeDtypeStruct((blocks // deep, 8 * deep + 8, LANES), F32)
    if slot_cap % LANES:
        slot_rows = send_index.reshape(blocks, LANES)
    else:
        slot_rows = send_index[0]
    outgoing, place, owner = pl.pallas_call(
        functools.partial(owner_kernel, sub_count, view_count, slot_cap),
        out_shape=(
            packet_shape,
            jax.ShapeDtypeStruct((2 * blocks, LANES), I32),
            jax.ShapeDtypeStruct((8, gauss_count), F32),
        ),
        in_specs=[IN_PLACE] * 5 + [IN_SMEM, IN_VMEM, IN_VMEM, IN_SMEM],
        out_specs=(IN_VMEM,) * 3,
        scratch_shapes=[
            pltpu.VMEM((blocks, LANES), I32),
            pltpu.VMEM((blocks, LANES), I32),
            pltpu.VMEM((16, gauss_count), F32),
            pltpu.VMEM(centers.shape, F32),
            pltpu.VMEM(scale_log.shape, F32),
            pltpu.VMEM(shear_terms.shape, F32),
            pltpu.VMEM(opacity_row.shape, F32),
            pltpu.VMEM(sh_coeffs.shape, F32),
            pltpu.SemaphoreType.DMA((5,)),
        ],
        compiler_params=PARAMS,
        name="owner_rows",
    )(*source, sh_coeffs, cameras, harmonics, slot_rows, send_count)
    arrived = exchange(outgoing, 0, peers, slot_cap)
    returning, rendered = pl.pallas_call(
        functools.partial(tile_kernel, slot_cap, peers, sub_count),
        out_shape=(
            packet_shape,
            jax.ShapeDtypeStruct((3, tiles, tile_pix), F32),
        ),
        in_specs=[IN_VMEM, IN_VMEM, IN_SMEM, IN_SMEM, IN_VMEM],
        out_specs=(IN_VMEM,) * 2,
        scratch_shapes=[
            pltpu.VMEM((9 * list_len // LANES, tiles, LANES), F32),
            pltpu.VMEM((list_len, tiles, tile_pix), F32),
            pltpu.VMEM((list_len, tiles, tile_pix), F32),
            pltpu.VMEM((16, tiles * list_len), F32),
            pltpu.VMEM((blocks, LANES), I32),
            pltpu.VMEM((blocks, LANES), I32),
        ],
        compiler_params=PARAMS,
        name="tile_blend",
    )(arrived, tile_list[0], tile_count, appearance, target[:, 0, 0])
    returned = exchange(returning, 1, peers, slot_cap)
    param_grad, appearance_grad = pl.pallas_call(
        functools.partial(
            gradient_kernel,
            sub_count,
            view_count,
            slot_cap,
            peers,
            float(tile_devs * sub_count * tiles * tile_pix),
        ),
        out_shape=(
            jax.ShapeDtypeStruct((10 + sh_coeffs.shape[0], gauss_count), F32),
            jax.ShapeDtypeStruct((1, 12), F32),
        ),
        in_specs=[IN_VMEM] * 4 + [IN_SMEM] + [IN_VMEM] * 4,
        out_specs=(IN_VMEM,) * 2,
        scratch_shapes=[
            pltpu.VMEM((16, gauss_count), F32),
            pltpu.VMEM((blocks, LANES), I32),
            pltpu.VMEM((blocks, LANES), I32),
        ],
        compiler_params=PARAMS,
        name="owner_gradient",
    )(*source, cameras, harmonics, place, owner, returned)
    return (rendered[:, None, None], param_grad, appearance_grad)


def solution(mesh):
    return jax.shard_map(
        on_device,
        mesh=mesh,
        in_specs=(
            P(None, ("group", "tile", "view", "sub")),
            P(None, ("group", "tile", "view", "sub")),
            P(None, ("group", "tile", "view", "sub")),
            P(("group", "tile", "view", "sub")),
            P(None, ("group", "tile", "view", "sub")),
            P("group", None),
            P(("group", "view"), None),
            P(None, ("group", "view"), ("tile", "sub"), None, None),
            P(("group", "tile", "view", "sub"), None, None),
            P(("group", "tile", "view", "sub"), None),
            P(("group", "tile", "view", "sub"), None, None),
            P(("group", "tile", "view", "sub"), None),
        ),
        out_specs=(
            P(None, ("group", "view"), ("tile", "sub"), None, None),
            P(None, ("group", "tile", "view", "sub")),
            P(("group", "view"), None),
        ),
        check_vma=False,
    )
```
